32 devices in a mesh: seq: 16 (over z, y, core), head: 2 (over x).
Axes of the slice: x: 2, y: 2, z: 4, core: 2. Of those that a mesh axis runs over, the one named last changes fastest.
Arguments:
- query: bfloat16 [4096, 3584], P('seq', 'head'), may hold values from -6 to 6
- key: bfloat16 [4096, 512], P('seq', 'head'), may hold values from -6 to 6
- value: bfloat16 [4096, 512], P('seq', 'head'), may hold values from -6 to 6
- output: bfloat16 [4096, 3584], P('seq', 'head'), may hold values from -6 to 6
- output_gradient: bfloat16 [4096, 3584], P('seq', 'head'), may hold values from -6 to 6
- lse: float32 [28, 4096], P('head', 'seq'), may hold values from 3 to 6
- doc_lengths: int32 [4], replicated, may hold values from 1 to 2048, as said below
- w_query: bfloat16 [3584, 3584], P('seq', 'head'), may hold values from -0.09375 to 0.09375
- key_weight: bfloat16 [3584, 512], P('seq', 'head'), may hold values from -0.09375 to 0.09375
- value_weight: bfloat16 [3584, 512], P('seq', 'head'), may hold values from -0.09375 to 0.09375
Outputs:
- grad_input: bfloat16 [4096, 3584], P('seq', 'head')
The draws below stay inside these ranges and needn't reach their ends.
Inputs may be any that keep to these rules, and one draw needn't show every extreme that they name: `doc_lengths`: the documents lie end to end and fill the 4096 tokens of the pack; the first has 1024 tokens, and one of exactly 2048 tokens begins at token 1024.
All inputs are finite; a program needn't handle non-finite values.
Results may differ from the reference program's by a relative error of at most 0.0056.
Values may be sent and summed in bfloat16 or wider, within the bound.
No kernel may reach another device: no remote copies, remote signals or barrier semaphores. Data moves between devices by JAX's collectives and lax.ppermute only.
A program may use at most 128 MiB of HBM per device.

```python
import math
import jax
import jax.numpy as jnp
from jax import lax

MODEL_WIDTH = 3584
HQ = 28
KEY_VALUE_HEADS = 4
HEAD_SIZE = 128
TOKENS_PER_SHARD = 256
QUERY_PER_KV = 7
WINDOW = 512
PACK_TOKENS = 4096
DOCS = 4
MAXDOC = 2048
N_SEQ = 16


def split_span(subkey, span, count):
    if count == 0:
        return jnp.zeros((0,), jnp.int32)
    if count == 1:
        return jnp.full((1,), span, jnp.int32)
    base = span // count
    shifts = jax.random.randint(subkey, (count - 1,), 0, base // 2 + 1, dtype=jnp.int32)
    zero_one = jnp.zeros((1,), jnp.int32)
    pieces = base + jnp.concatenate([shifts, zero_one]) - jnp.concatenate([zero_one, shifts])
    extra = jnp.concatenate([jnp.zeros((count - 1,), jnp.int32), jnp.full((1,), span - count * base, jnp.int32)])
    return pieces + extra


def draw_doc_lengths(key, part):
    blocks = PACK_TOKENS // TOKENS_PER_SHARD
    half_blocks = blocks // 2
    first_span = (half_blocks - 8) * TOKENS_PER_SHARD
    second_span = (half_blocks - 4) * TOKENS_PER_SHARD
    first_count = (half_blocks - 8) // 4
    second_count = DOCS - 2 - first_count
    first_part = split_span(jax.random.fold_in(key, 11), first_span, first_count)
    second_part = split_span(jax.random.fold_in(key, 23), second_span, second_count)
    head_doc = jnp.full((1,), 4 * TOKENS_PER_SHARD, jnp.int32)
    long_doc = jnp.full((1,), MAXDOC, jnp.int32)
    return jnp.concatenate([head_doc, first_part, long_doc, second_part]).astype(jnp.int32)


def block_levels(rng, shape, split, least, largest):
    loudness = 1.0
    for dim, parts in split:
        draws = jax.random.uniform(jax.random.fold_in(jax.random.fold_in(rng, 6), dim), (parts,), jnp.float32, least / len(split), largest / len(split))
        loudness = loudness * jnp.repeat(jnp.exp(draws), shape[dim] // parts).reshape((-1,) + (1,) * (len(shape) - 1 - dim))
    return loudness


def normal_values(stream_key, extent, deviation, bound, cuts=(), kind=jnp.bfloat16):
    entries = deviation * jax.random.normal(stream_key, extent, jnp.float32)
    if cuts:
        entries = entries * block_levels(stream_key, extent, cuts, -0.22, 0.18)
    return jnp.clip(entries, -bound, bound).astype(kind)


def setup_inputs(seed: int = 0) -> dict:
    key_list = jax.random.split(jax.random.key(seed), 11)
    query = normal_values(key_list[0], (PACK_TOKENS, HQ * HEAD_SIZE), 1.0, 6.0, ((0, 16), (1, 2)))
    key = normal_values(key_list[1], (PACK_TOKENS, KEY_VALUE_HEADS * HEAD_SIZE), 1.0, 6.0, ((0, 16), (1, 2)))
    value = normal_values(key_list[2], (PACK_TOKENS, KEY_VALUE_HEADS * HEAD_SIZE), 1.0, 6.0, ((0, 16), (1, 2)))
    output = normal_values(key_list[3], (PACK_TOKENS, HQ * HEAD_SIZE), 1.0, 6.0, ((0, 16), (1, 2)))
    output_gradient = normal_values(key_list[4], (PACK_TOKENS, HQ * HEAD_SIZE), 1.0, 6.0, ((0, 16), (1, 2)))
    lse = jnp.clip(3.0 + 3.0 * jax.random.uniform(key_list[5], (HQ, PACK_TOKENS), jnp.float32) ** block_levels(key_list[5], (HQ, PACK_TOKENS), ((0, 2), (1, 16)), -0.2, 0.2), 3.0, 6.0)
    doc_lengths = draw_doc_lengths(jax.random.fold_in(key_list[10], 71), 0)
    w_query = normal_values(key_list[7], (MODEL_WIDTH, HQ * HEAD_SIZE), MODEL_WIDTH ** -0.5, 0.09375, ((0, 16), (1, 2)))
    key_weight = normal_values(key_list[8], (MODEL_WIDTH, KEY_VALUE_HEADS * HEAD_SIZE), MODEL_WIDTH ** -0.5, 0.09375, ((0, 16), (1, 2)))
    value_weight = normal_values(key_list[9], (MODEL_WIDTH, KEY_VALUE_HEADS * HEAD_SIZE), MODEL_WIDTH ** -0.5, 0.09375, ((0, 16), (1, 2)))
    return dict(query=query, key=key, value=value, output=output, output_gradient=output_gradient, lse=lse, doc_lengths=doc_lengths, w_query=w_query, key_weight=key_weight, value_weight=value_weight)


def lower_bounds(positions, doc_lengths, window):
    starts = jnp.cumsum(doc_lengths, dtype=jnp.int32) - doc_lengths
    inside = starts[None, :] <= positions[:, None]
    doc_begin = lax.optimization_barrier(jnp.max(jnp.where(inside, starts[None, :], 0), axis=1))
    return jnp.maximum(doc_begin, positions - window + 1)

def attend(query_rows, key_row_block, value_row_block, visible, logsumexp_rows, output_grad_rows, row_delta, score_scale):
    q_full = query_rows.astype(jnp.float32)
    k_full = key_row_block.astype(jnp.float32)
    v_full = value_row_block.astype(jnp.float32)
    g_full = output_grad_rows.astype(jnp.float32)
    scores = jnp.einsum('tgjd,kgd->gjtk', q_full, k_full) * score_scale
    prob_full = jnp.where(visible[None, None], jnp.exp(scores - logsumexp_rows[..., None]), 0.0)
    prob_low = prob_full.astype(jnp.bfloat16)
    grad_val = jnp.einsum('gjtk,tgjd->kgd', prob_low.astype(jnp.float32), g_full)
    grad_prob = jnp.einsum('tgjd,kgd->gjtk', g_full, v_full)
    dscore = (prob_full * (grad_prob - row_delta[..., None]) * score_scale).astype(jnp.bfloat16)
    dscore_full = dscore.astype(jnp.float32)
    grad_qry = jnp.einsum('gjtk,kgd->tgjd', dscore_full, k_full)
    grad_key = jnp.einsum('gjtk,tgjd->kgd', dscore_full, q_full)
    return (grad_qry, grad_key, grad_val)

def reference(query, key, value, output, output_gradient, lse, doc_lengths, w_query, key_weight, value_weight):
    key_value_width = KEY_VALUE_HEADS * HEAD_SIZE
    score_scale = 1.0 / math.sqrt(HEAD_SIZE)
    pad_rows = 2 * TOKENS_PER_SHARD
    padded_keys = jnp.concatenate([jnp.zeros((pad_rows, key_value_width), key.dtype), key], 0)
    padded_values = jnp.concatenate([jnp.zeros((pad_rows, key_value_width), value.dtype), value], 0)

    def step(carry, block_idx):
        key_acc, value_acc = carry
        first_index = block_idx * TOKENS_PER_SHARD
        positions = first_index + jnp.arange(TOKENS_PER_SHARD, dtype=jnp.int32)
        lower = lower_bounds(positions, doc_lengths, WINDOW)
        key_pos = first_index - pad_rows + jnp.arange(3 * TOKENS_PER_SHARD, dtype=jnp.int32)
        visible = (key_pos[None, :] >= lower[:, None]) & (key_pos[None, :] <= positions[:, None])
        query_rows = lax.dynamic_slice_in_dim(query, first_index, TOKENS_PER_SHARD, 0).reshape(TOKENS_PER_SHARD, KEY_VALUE_HEADS, QUERY_PER_KV, HEAD_SIZE)
        output_rows = lax.dynamic_slice_in_dim(output, first_index, TOKENS_PER_SHARD, 0).reshape(TOKENS_PER_SHARD, KEY_VALUE_HEADS, QUERY_PER_KV, HEAD_SIZE)
        output_grad_rows = lax.dynamic_slice_in_dim(output_gradient, first_index, TOKENS_PER_SHARD, 0).reshape(TOKENS_PER_SHARD, KEY_VALUE_HEADS, QUERY_PER_KV, HEAD_SIZE)
        key_row_block = lax.dynamic_slice_in_dim(padded_keys, first_index, 3 * TOKENS_PER_SHARD, 0).reshape(3 * TOKENS_PER_SHARD, KEY_VALUE_HEADS, HEAD_SIZE)
        value_row_block = lax.dynamic_slice_in_dim(padded_values, first_index, 3 * TOKENS_PER_SHARD, 0).reshape(3 * TOKENS_PER_SHARD, KEY_VALUE_HEADS, HEAD_SIZE)
        logsumexp_rows = lax.dynamic_slice_in_dim(lse, first_index, TOKENS_PER_SHARD, 1).reshape(KEY_VALUE_HEADS, QUERY_PER_KV, TOKENS_PER_SHARD)
        row_delta = jnp.einsum('tgjd,tgjd->gjt', output_grad_rows.astype(jnp.float32), output_rows.astype(jnp.float32))
        grad_qry, grad_key, grad_val = attend(query_rows, key_row_block, value_row_block, visible, logsumexp_rows, output_grad_rows, row_delta, score_scale)
        old_key = lax.dynamic_slice_in_dim(key_acc, first_index, 3 * TOKENS_PER_SHARD, 0)
        old_value = lax.dynamic_slice_in_dim(value_acc, first_index, 3 * TOKENS_PER_SHARD, 0)
        key_acc = lax.dynamic_update_slice_in_dim(key_acc, old_key + grad_key.reshape(3 * TOKENS_PER_SHARD, key_value_width), first_index, 0)
        value_acc = lax.dynamic_update_slice_in_dim(value_acc, old_value + grad_val.reshape(3 * TOKENS_PER_SHARD, key_value_width), first_index, 0)
        return ((key_acc, value_acc), grad_qry.reshape(TOKENS_PER_SHARD, HQ * HEAD_SIZE).astype(jnp.bfloat16))
    zero_acc = jnp.zeros((PACK_TOKENS + pad_rows, key_value_width), jnp.float32)
    (key_acc, value_acc), q_blocks = lax.scan(step, (zero_acc, zero_acc), jnp.arange(N_SEQ, dtype=jnp.int32))
    grad_query = q_blocks.reshape(PACK_TOKENS, HQ * HEAD_SIZE)
    grad_key = key_acc[pad_rows:].astype(jnp.bfloat16)
    grad_value = value_acc[pad_rows:].astype(jnp.bfloat16)
    total = jnp.dot(grad_query, w_query.T, preferred_element_type=jnp.float32)
    total = total + jnp.dot(grad_key, key_weight.T, preferred_element_type=jnp.float32)
    total = total + jnp.dot(grad_value, value_weight.T, preferred_element_type=jnp.float32)
    return total.astype(jnp.bfloat16)
```

```python
import math

import jax
import jax.numpy as jnp
from jax import lax
from jax.experimental import pallas as pl
from jax.experimental.pallas import tpu as pltpu
from jax.sharding import PartitionSpec as P

HEAD_SIZE = 128
WINDOW = 512
INNER = 4
LOG2E = 1.4426950408889634
F32 = jnp.float32
BF16 = jnp.bfloat16


def attention_kernel(
    first_ref, docs_ref, q_ref, do_ref, o_ref, lse_ref,
    k_own_ref, v_own_ref, k_near_ref, v_near_ref, k_far_ref, v_far_ref,
    dq_ref, own_ref, near_ref, far_ref,
    bias_ref, acc_k, acc_v,
):
    tokens = k_own_ref.shape[0]
    per_group = q_ref.shape[1] // HEAD_SIZE
    group = pl.program_id(0)
    groups = own_ref.shape[1] // (2 * HEAD_SIZE)
    scale = 1.0 / math.sqrt(HEAD_SIZE)
    rows = lax.broadcasted_iota(jnp.int32, (tokens, tokens), 0)
    cols = lax.broadcasted_iota(jnp.int32, (tokens, tokens), 1)
    causal = rows <= cols

    @pl.when(group == 0)
    def _():
        first = first_ref[0]
        spot = first + lax.broadcasted_iota(jnp.int32, (8, tokens), 1)
        start = jnp.int32(0)
        doc_begin = jnp.zeros((8, tokens), jnp.int32)
        for d in range(docs_ref.shape[0]):
            doc_begin = jnp.maximum(doc_begin, jnp.where(start <= spot, start, 0))
            start = start + docs_ref[d]
        doc_row = doc_begin[0:1]
        mixed = first + rows - jnp.where(causal, 0, 2 * tokens)
        near = first - tokens + rows
        bias_ref[0] = jnp.where(mixed >= doc_row, 0.0, -1e30)
        bias_ref[1] = jnp.where(near >= doc_row, 0.0, -1e30)

    nt = (((1,), (1,)), ((), ()))
    tn = (((0,), (0,)), ((), ()))

    def dot(a, b, dims=(((1,), (0,)), ((), ()))):
        return lax.dot_general(a, b, dims, preferred_element_type=F32)

    k_own, k_near, k_far = k_own_ref[...], k_near_ref[...], k_far_ref[...]
    v_own, v_near, v_far = v_own_ref[...], v_near_ref[...], v_far_ref[...]
    for j in range(per_group):
        span = slice(j * HEAD_SIZE, (j + 1) * HEAD_SIZE)
        q, do, o = q_ref[:, span], do_ref[:, span], o_ref[:, span]
        lse2 = lse_ref[pl.ds(group * per_group + j, 1), :] * LOG2E
        delta = jnp.sum((do.astype(F32) * o.astype(F32)).T, axis=0, keepdims=True)

        def prob(scores, bias):
            return jnp.exp2(scores * (scale * LOG2E) - lse2 + bias)

        p_mix = prob(jnp.where(causal, dot(k_own, q, nt), dot(k_far, q, nt)), bias_ref[0])
        p_near = prob(dot(k_near, q, nt), bias_ref[1])
        g_mix = jnp.where(causal, dot(v_own, do, nt), dot(v_far, do, nt))
        g_near = dot(v_near, do, nt)
        ds_mix = p_mix * (g_mix - delta) * scale
        ds_near = (p_near * (g_near - delta) * scale).astype(BF16)
        zero = jnp.zeros_like(p_mix)
        ds_own = jnp.where(causal, ds_mix, zero).astype(BF16)
        ds_far = jnp.where(causal, zero, ds_mix).astype(BF16)
        p_own = jnp.where(causal, p_mix, zero).astype(BF16)
        p_far = jnp.where(causal, zero, p_mix).astype(BF16)
        p_near = p_near.astype(BF16)
        dq = dot(ds_own, k_own, tn) + dot(ds_near, k_near, tn) + dot(ds_far, k_far, tn)
        dq_ref[:, span] = dq.astype(BF16)
        for i, (p, ds) in enumerate(((p_own, ds_own), (p_near, ds_near), (p_far, ds_far))):
            dv, dk = dot(p, do), dot(ds, q)
            if j == 0:
                acc_v[i], acc_k[i] = dv, dk
            else:
                acc_v[i] += dv
                acc_k[i] += dk
    k_cols = pl.ds(pl.multiple_of(group * HEAD_SIZE, HEAD_SIZE), HEAD_SIZE)
    v_cols = pl.ds(pl.multiple_of((groups + group) * HEAD_SIZE, HEAD_SIZE), HEAD_SIZE)
    for i, ref in enumerate((own_ref, near_ref, far_ref)):
        ref[:, k_cols] = acc_k[i].astype(ref.dtype)
        ref[:, v_cols] = acc_v[i].astype(ref.dtype)


def attention(first, doc_lengths, query, output_gradient, output, lse, own, near, far):
    tokens, width = query.shape
    kv_width = own.shape[1]
    groups = kv_width // (2 * HEAD_SIZE)
    wide = pl.BlockSpec((tokens, width // groups), lambda g: (0, g))
    smem = pl.BlockSpec(memory_space=pltpu.SMEM)
    k_spec = pl.BlockSpec((tokens, HEAD_SIZE), lambda g: (0, g))
    v_spec = pl.BlockSpec((tokens, HEAD_SIZE), lambda g: (0, groups + g))
    whole = pl.BlockSpec((tokens, kv_width), lambda g: (0, 0))
    return pl.pallas_call(
        attention_kernel,
        grid=(groups,),
        in_specs=[smem, smem, wide, wide, wide, pl.BlockSpec(lse.shape, lambda g: (0, 0))]
        + [k_spec, v_spec] * 3,
        out_specs=[wide, whole, whole, whole],
        out_shape=[
            jax.ShapeDtypeStruct((tokens, width), BF16),
            jax.ShapeDtypeStruct((tokens, kv_width), F32),
            jax.ShapeDtypeStruct((tokens, kv_width), BF16),
            jax.ShapeDtypeStruct((tokens, kv_width), BF16),
        ],
        scratch_shapes=[
            pltpu.VMEM((2, tokens, tokens), F32),
            pltpu.VMEM((3, tokens, HEAD_SIZE), F32),
            pltpu.VMEM((3, tokens, HEAD_SIZE), F32),
        ],
        compiler_params=pltpu.CompilerParams(vmem_limit_bytes=48 * 2**20),
        name="attention",
    )(first, doc_lengths, query, output_gradient, output, lse, own, own, near, near, far, far)


def project_kernel(pick_ref, grad_ref, *refs):
    shards, out_ref, weight, sem = refs[:-3], refs[-3], refs[-2], refs[-1]

    @pl.when(pl.program_id(0) == 0)
    def _():
        for i, shard in enumerate(shards):
            @pl.when(pick_ref[0] == i)
            def _():
                copy = pltpu.make_async_copy(shard, weight, sem)
                copy.start()
                copy.wait()

    out_ref[...] = lax.dot_general(
        grad_ref[...], weight[...], (((1,), (1,)), ((), ())), preferred_element_type=F32
    ).astype(out_ref.dtype)


def project(pick, grads, shards, dtype):
    tokens, depth = grads.shape
    cols = shards[0].shape[0]
    block = tokens // INNER
    return pl.pallas_call(
        project_kernel,
        grid=(INNER,),
        in_specs=[
            pl.BlockSpec(memory_space=pltpu.SMEM),
            pl.BlockSpec((block, depth), lambda t: (t, 0)),
        ]
        + [pl.BlockSpec(memory_space=pl.ANY)] * len(shards),
        out_specs=pl.BlockSpec((block, cols), lambda t: (t, 0)),
        out_shape=jax.ShapeDtypeStruct((tokens, cols), dtype),
        scratch_shapes=[pltpu.VMEM(shards[0].shape, BF16), pltpu.SemaphoreType.DMA],
        compiler_params=pltpu.CompilerParams(vmem_limit_bytes=32 * 2**20),
        name="project",
    )(pick.reshape(1).astype(jnp.int32), grads, *shards)


def shifted(array, by):
    peers = lax.axis_size("seq")
    pairs = [(i, i + by) for i in range(peers) if 0 <= i + by < peers]
    return lax.ppermute(array, "seq", pairs)


def swapped(array, bits):
    peers = lax.axis_size("seq")
    return lax.ppermute(array, "seq", [(i, i ^ bits) for i in range(peers)])


def layered(array, moves):
    pairs = [(a * INNER + i, b * INNER + i) for a, b in moves for i in range(INNER)]
    return lax.ppermute(array, "seq", pairs)


def returned(done, tokens):
    blocks = done.reshape(INNER, tokens, -1)
    return [blocks[0], swapped(blocks[2], 1), swapped(blocks[1], 2), swapped(blocks[3], 3)]


def ordered(blocks, inner):
    cols = []
    for j in range(INNER):
        pick = blocks[j]
        for i in range(1, INNER):
            pick = jnp.where(inner == i, blocks[j ^ i], pick)
        cols.append(pick)
    return jnp.concatenate(cols, 1)


def project_gathered(grads, weight, layers, tokens, head, inner):
    rows = weight.shape[0]
    groups = [[z * INNER + i for z in range(layers)] for i in range(INNER)]
    every = lax.all_gather(weight, "seq", axis=0, tiled=True, axis_index_groups=groups)
    halves = every.reshape(2, layers // 2 * rows, -1)

    def times(piece):
        return lax.dot_general(
            grads, piece, (((1,), (1,)), ((), ())), preferred_element_type=F32
        )

    send = times(jnp.where(head == 0, halves[1], halves[0])).astype(BF16)
    got = lax.ppermute(send, "head", [(0, 1), (1, 0)])
    keep = times(jnp.where(head == 0, halves[0], halves[1]))
    blocks = returned((keep + got.astype(F32)).astype(BF16), tokens)
    blocks = [b.reshape(tokens * (layers // 2), rows) for b in blocks]
    return ordered(blocks, inner).reshape(tokens, -1)


def shards(
    query, key, value, output, output_gradient, lse, doc_lengths, w_query, key_weight, value_weight
):
    tokens = query.shape[0]
    seq = lax.axis_index("seq")
    head = lax.axis_index("head")
    layer, inner = seq // INNER, seq % INNER
    layers = lax.axis_size("seq") // INNER
    half = layer // (layers // 2)

    weight = jnp.concatenate([w_query, key_weight, value_weight], 1)
    pair = jnp.concatenate([key, value], 1)
    near = shifted(pair, 1)
    far = shifted(pair, 2)
    if layers == 4:
        mate = layered(weight, [(0, 1), (1, 0), (2, 3), (3, 2)])
        mid = layered(weight, [(1, 2), (2, 1)])
        edge_third = layered(mid, [(1, 0), (2, 3)])
        mid_fourth = layered(mate, [(1, 2), (2, 1)])
        edge_fourth = layered(mid_fourth, [(1, 0), (2, 3)])

    first = (seq * tokens).astype(jnp.int32).reshape(1)
    dq, own_part, near_part, far_part = attention(
        first, doc_lengths, query, output_gradient, output, lse, pair, near, far
    )
    back_near = shifted(near_part, -1)
    back_far = shifted(far_part, -2)
    pair_grad = (own_part + back_near.astype(F32) + back_far.astype(F32)).astype(BF16)
    grads = jnp.concatenate([dq, pair_grad], 1)
    two = jnp.concatenate([grads, swapped(grads, 2)], 0)
    four = jnp.concatenate([two, swapped(two, 1)], 0)

    if layers != 4:
        return project_gathered(four, weight, layers, tokens, head, inner)

    is_edge = (layer == 0) | (layer == 3)
    same = head == half
    third = jnp.where(is_edge, 1, 2)
    fourth = jnp.where(is_edge, 1, 2)
    set_a = (weight, edge_third, mid)
    set_b = (mate, edge_fourth, mid_fourth)

    def finish(a_set, other):
        send = project(jnp.where(same, other, 0), four, a_set, BF16)
        got = lax.ppermute(send, "head", [(0, 1), (1, 0)])
        keep = project(jnp.where(same, 0, other), four, a_set, F32)
        return returned((keep + got.astype(F32)).astype(BF16), tokens)

    part_a = finish(set_a, third)
    part_b = finish(set_b, fourth)

    part_a, part_b = ordered(part_a, inner), ordered(part_b, inner)
    a_first = jnp.where(same, layer % 2 == 0, half == 0)
    return jnp.where(
        a_first,
        jnp.concatenate([part_a, part_b], 1),
        jnp.concatenate([part_b, part_a], 1),
    )


def solution(mesh):
    in_specs = (
        P("seq", "head"),
        P("seq", "head"),
        P("seq", "head"),
        P("seq", "head"),
        P("seq", "head"),
        P("head", "seq"),
        P(),
        P("seq", "head"),
        P("seq", "head"),
        P("seq", "head"),
    )
    out_specs = P("seq", "head")
    return jax.shard_map(shards, mesh=mesh, in_specs=in_specs, out_specs=out_specs, check_vma=False)
```

```python
import functools
import math

import jax
import jax.numpy as jnp
from jax import lax
from jax.experimental import pallas as pl
from jax.experimental.pallas import tpu as pltpu
from jax.sharding import PartitionSpec as P

HEAD_SIZE = 128
WINDOW = 512
INNER = 4
LOG2E = 1.4426950408889634
VMEM_LIMIT = 63 * 2**20
F32 = jnp.float32
BF16 = jnp.bfloat16


def attention_kernel(
    group, groups, first_ref, docs_ref, q_ref, do_ref, o_ref, lse_ref,
    k_own_ref, v_own_ref, k_near_ref, v_near_ref, k_far_ref, v_far_ref,
    *refs,
):
    *earlier, dq_ref, own_ref, near_ref, far_ref, acc_k, acc_v = refs
    tokens = k_own_ref.shape[0]
    per_group = q_ref.shape[1] // HEAD_SIZE
    scale = 1.0 / math.sqrt(HEAD_SIZE)
    rows = lax.broadcasted_iota(jnp.int32, (tokens, tokens), 0)
    cols = lax.broadcasted_iota(jnp.int32, (tokens, tokens), 1)
    causal = rows <= cols
    first = first_ref[0]
    spot = first + lax.broadcasted_iota(jnp.int32, (8, tokens), 1)
    start = jnp.int32(0)
    doc_begin = jnp.zeros((8, tokens), jnp.int32)
    for d in range(docs_ref.shape[0]):
        doc_begin = jnp.maximum(doc_begin, jnp.where(start <= spot, start, 0))
        start = start + docs_ref[d]
    doc_row = doc_begin[0:1]
    mixed = first + rows - jnp.where(causal, 0, 2 * tokens)
    bias_mix = jnp.where(mixed >= doc_row, 0.0, -1e30)
    bias_near = jnp.where(first - tokens + rows >= doc_row, 0.0, -1e30)

    nt = (((1,), (1,)), ((), ()))
    tn = (((0,), (0,)), ((), ()))

    def dot(a, b, dims=(((1,), (0,)), ((), ()))):
        return lax.dot_general(a, b, dims, preferred_element_type=F32)

    k_own, k_near, k_far = k_own_ref[...], k_near_ref[...], k_far_ref[...]
    v_own, v_near, v_far = v_own_ref[...], v_near_ref[...], v_far_ref[...]
    for j in range(per_group):
        span = slice(j * HEAD_SIZE, (j + 1) * HEAD_SIZE)
        q, do, o = q_ref[:, span], do_ref[:, span], o_ref[:, span]
        head = group * per_group + j
        lse2 = lse_ref[head : head + 1, :] * LOG2E
        delta = jnp.sum((do.astype(F32) * o.astype(F32)).T, axis=0, keepdims=True)

        def prob(scores, bias):
            return jnp.exp2(scores * (scale * LOG2E) - lse2 + bias)

        p_mix = prob(jnp.where(causal, dot(k_own, q, nt), dot(k_far, q, nt)), bias_mix)
        p_near = prob(dot(k_near, q, nt), bias_near)
        g_mix = jnp.where(causal, dot(v_own, do, nt), dot(v_far, do, nt))
        g_near = dot(v_near, do, nt)
        ds_mix = p_mix * (g_mix - delta) * scale
        ds_near = (p_near * (g_near - delta) * scale).astype(BF16)
        zero = jnp.zeros_like(p_mix)
        ds_own = jnp.where(causal, ds_mix, zero).astype(BF16)
        ds_far = jnp.where(causal, zero, ds_mix).astype(BF16)
        p_own = jnp.where(causal, p_mix, zero).astype(BF16)
        p_far = jnp.where(causal, zero, p_mix).astype(BF16)
        p_near = p_near.astype(BF16)
        dq = dot(ds_own, k_own, tn) + dot(ds_near, k_near, tn) + dot(ds_far, k_far, tn)
        dq_ref[:, span] = dq.astype(BF16)
        for i, (p, ds) in enumerate(((p_own, ds_own), (p_near, ds_near), (p_far, ds_far))):
            dv, dk = dot(p, do), dot(ds, q)
            if j == 0:
                acc_v[i], acc_k[i] = dv, dk
            else:
                acc_v[i] += dv
                acc_k[i] += dk
    for i, ref in enumerate((own_ref, near_ref, far_ref)):
        if group < groups - 1:
            ref[:, :HEAD_SIZE] = acc_k[i].astype(ref.dtype)
            ref[:, HEAD_SIZE:] = acc_v[i].astype(ref.dtype)
            continue
        for g in range(groups):
            k_cols = slice(g * HEAD_SIZE, (g + 1) * HEAD_SIZE)
            v_cols = slice((groups + g) * HEAD_SIZE, (groups + g + 1) * HEAD_SIZE)
            if g == group:
                ref[:, k_cols] = acc_k[i].astype(ref.dtype)
                ref[:, v_cols] = acc_v[i].astype(ref.dtype)
            else:
                ref[:, k_cols] = earlier[3 * g + i][:, :HEAD_SIZE]
                ref[:, v_cols] = earlier[3 * g + i][:, HEAD_SIZE:]


def attention(group, cost, first, doc_lengths, query, output_gradient, output, lse, own, near, far, earlier):
    tokens, width = query.shape
    groups = own.shape[1] // (2 * HEAD_SIZE)
    kv_width = own.shape[1] if group == groups - 1 else 2 * HEAD_SIZE
    part = width // groups
    wide = pl.BlockSpec((tokens, part), lambda i: (0, group))
    smem = pl.BlockSpec(memory_space=pltpu.SMEM)
    k_spec = pl.BlockSpec((tokens, HEAD_SIZE), lambda i: (0, group))
    v_spec = pl.BlockSpec((tokens, HEAD_SIZE), lambda i: (0, groups + group))

    def whole(shape):
        return pl.BlockSpec(shape, lambda i: (0, 0))

    return pl.pallas_call(
        functools.partial(attention_kernel, group, groups),
        grid=(1,),
        in_specs=[smem, smem, wide, wide, wide, whole(lse.shape)]
        + [k_spec, v_spec] * 3
        + [whole(array.shape) for array in earlier],
        out_specs=[whole((tokens, part))] + [whole((tokens, kv_width))] * 3,
        out_shape=[
            jax.ShapeDtypeStruct((tokens, part), BF16),
            jax.ShapeDtypeStruct((tokens, kv_width), F32),
            jax.ShapeDtypeStruct((tokens, kv_width), BF16),
            jax.ShapeDtypeStruct((tokens, kv_width), BF16),
        ],
        scratch_shapes=[
            pltpu.VMEM((3, tokens, HEAD_SIZE), F32),
            pltpu.VMEM((3, tokens, HEAD_SIZE), F32),
        ],
        compiler_params=pltpu.CompilerParams(vmem_limit_bytes=VMEM_LIMIT),
        cost_estimate=pl.CostEstimate(flops=cost, transcendentals=0, bytes_accessed=1),
        name="attention",
    )(
        first, doc_lengths, query, output_gradient, output, lse,
        own, own, near, near, far, far, *earlier,
    )


NT = (((1,), (1,)), ((), ()))


def grad_copies(grads, held, sems):
    parts = len(grads) // INNER
    tokens = grads[0].shape[0]
    copies = []
    for t in range(INNER):
        lane = 0
        copies.append([])
        for i, grad in enumerate(grads[t * parts : (t + 1) * parts]):
            width = grad.shape[1]
            copies[-1].append(pltpu.make_async_copy(
                grad,
                held.at[t * tokens : (t + 1) * tokens, lane : lane + width],
                sems.at[t * parts + i],
            ))
            lane += width
    for t in range(2):
        for copy in copies[t]:
            copy.start()

    def ready(t):
        for copy in copies[t]:
            copy.wait()
        if t + 2 < INNER:
            for copy in copies[t + 2]:
                copy.start()

    return ready


def standing(layers):
    layer = lax.axis_index("seq") // INNER
    at_edge = (layer == 0) | (layer == layers - 1)
    return at_edge, lax.axis_index("head") == layer // (layers // 2)


def fetch_either(choice, first, second, weight, sem):
    @pl.when(choice)
    def _():
        pltpu.make_async_copy(first, weight, sem).start()

    @pl.when(jnp.logical_not(choice))
    def _():
        pltpu.make_async_copy(second, weight, sem).start()


def times(grad, weight):
    return lax.dot_general(grad, weight, NT, preferred_element_type=F32)


def send_kernel(layers, count, *refs):
    grads, (own, edge, mid) = refs[:count], refs[count : count + 3]
    send, gathered, held, weight, sems = refs[-5:]
    tokens, cols = grads[0].shape[0], weight.shape[0]
    at_edge, same = standing(layers)

    @pl.when(same)
    def _():
        fetch_either(at_edge, edge, mid, weight, sems.at[count])

    @pl.when(jnp.logical_not(same))
    def _():
        pltpu.make_async_copy(own, weight, sems.at[count]).start()

    ready = grad_copies(grads, held, sems)
    pltpu.make_async_copy(own, weight, sems.at[count]).wait()
    stores = []
    for t in range(INNER):
        ready(t)
        rows = slice(t * tokens, (t + 1) * tokens)
        stores.append(pltpu.make_async_copy(
            held.at[rows], gathered.at[rows], sems.at[count + 1 + t]
        ))
        stores[-1].start()
        lanes = slice(t * cols, (t + 1) * cols)
        send[:, lanes] = times(held[rows, :], weight[...]).astype(BF16)
    for store in stores:
        store.wait()


def keep_kernel(layers, gathered, own, mate, edge, mid, *refs):
    keep, mate_full, mate_low, held, weights, sems = refs[-6:]
    cols = weights.shape[1]
    tokens = held.shape[0] // INNER
    at_edge, same = standing(layers)
    mate_copy = pltpu.make_async_copy(mate, weights.at[1], sems.at[INNER + 1])
    mate_copy.start()
    copies = []
    for t in range(INNER):
        rows = slice(t * tokens, (t + 1) * tokens)
        copies.append(pltpu.make_async_copy(gathered.at[rows], held.at[rows], sems.at[t]))
        copies[-1].start()

    @pl.when(same)
    def _():
        pltpu.make_async_copy(own, weights.at[0], sems.at[INNER]).start()

    @pl.when(jnp.logical_not(same))
    def _():
        fetch_either(at_edge, edge, mid, weights.at[0], sems.at[INNER])

    mate_copy.wait()
    for t in range(INNER):
        copies[t].wait()
        product = times(held[t * tokens : (t + 1) * tokens, :], weights[1])
        mate_full[t] = product
        mate_low[:, t * cols : (t + 1) * cols] = product.astype(BF16)
    pltpu.make_async_copy(own, weights.at[0], sems.at[INNER]).wait()
    for t in range(INNER):
        keep[t] = times(held[t * tokens : (t + 1) * tokens, :], weights[0])


def last_kernel(layers, held, piece, passed, *refs):
    full, low_first, low_second, weight, sem = refs[-5:]
    at_edge, _ = standing(layers)
    fetch_either(at_edge, piece, passed, weight, sem)
    pltpu.make_async_copy(piece, weight, sem).wait()
    tokens, cols = held.shape[0] // INNER, weight.shape[0]
    for t in range(INNER):
        product = times(held[t * tokens : (t + 1) * tokens, :], weight[...])
        full[t] = product
        low = low_first if t % 2 else low_second
        low[:, t // 2 * cols : (t // 2 + 1) * cols] = product.astype(BF16)


def project(kernel, layers, operands, in_vmem, outs, scratch, limit, name):
    vmem = pl.BlockSpec(memory_space=pltpu.VMEM)
    hbm = pl.BlockSpec(memory_space=pltpu.HBM)
    return pl.pallas_call(
        functools.partial(kernel, layers),
        in_specs=[vmem] * in_vmem + [hbm] * (len(operands) - in_vmem),
        out_specs=[vmem if in_place else hbm for in_place, _, _ in outs],
        out_shape=[jax.ShapeDtypeStruct(shape, kind) for _, shape, kind in outs],
        scratch_shapes=scratch,
        compiler_params=pltpu.CompilerParams(vmem_limit_bytes=limit),
        cost_estimate=pl.CostEstimate(flops=1, transcendentals=0, bytes_accessed=1),
        name=name,
    )(*operands)


def project_send(layers, grads, own, edge, mid):
    tokens = grads[0].shape[0]
    cols, depth = own.shape
    return project(
        lambda layers, *refs: send_kernel(layers, len(grads), *refs),
        layers,
        [*grads, own, edge, mid],
        0,
        [(True, (tokens, INNER * cols), BF16), (False, (INNER * tokens, depth), BF16)],
        [
            pltpu.VMEM((INNER * tokens, depth), BF16),
            pltpu.VMEM((cols, depth), BF16),
            pltpu.SemaphoreType.DMA((len(grads) + 1 + INNER,)),
        ],
        VMEM_LIMIT,
        "project_send",
    )


def project_keep(layers, gathered, own, mate, edge, mid, after):
    tokens, depth = gathered.shape[0] // INNER, gathered.shape[1]
    cols = own.shape[0]
    full = (True, (INNER, tokens, cols), F32)
    return project(
        keep_kernel,
        layers,
        [gathered, own, mate, edge, mid, *after],
        0,
        [full, full, (True, (tokens, INNER * cols), BF16)],
        [
            pltpu.VMEM((INNER * tokens, depth), BF16),
            pltpu.VMEM((2, cols, depth), BF16),
            pltpu.SemaphoreType.DMA((INNER + 2,)),
        ],
        VMEM_LIMIT,
        "project_keep",
    )


def project_last(layers, gathered, piece, passed, after):
    tokens, cols = gathered.shape[0] // INNER, piece.shape[0]
    low = (True, (tokens, INNER // 2 * cols), BF16)
    return project(
        last_kernel,
        layers,
        [gathered, piece, passed, *after],
        1,
        [(True, (INNER, tokens, cols), F32), low, low],
        [pltpu.VMEM(piece.shape, BF16), pltpu.SemaphoreType.DMA],
        10 * 2**20,
        "project_last",
    )


def place_kernel(flags, *refs):
    blocks, out = refs[:-1], refs[-1]
    sets = [blocks[k * INNER : (k + 1) * INNER] for k in range(len(blocks) // INNER)]
    width = sets[0][0].shape[1]
    for inner in range(INNER):
        for a_first in range(2):
            @pl.when((flags[0] == inner) & (flags[1] == a_first))
            def _():
                for j in range(INNER):
                    lanes = [(1 - a_first) * INNER * width + j * width]
                    lanes.append(a_first * INNER * width + j * width)
                    for cols in [each[0].shape[1] for each in sets[1:-1]]:
                        lanes.append(lanes[-1] + cols)
                    for lane, each in zip(lanes, sets):
                        block = each[j ^ inner]
                        out[:, lane : lane + block.shape[1]] = block[...]


def place(flags, sets):
    tokens, width = sets[0][0].shape
    blocks = [block for each in sets for block in each]
    vmem = pl.BlockSpec(memory_space=pltpu.VMEM)
    return pl.pallas_call(
        place_kernel,
        in_specs=[pl.BlockSpec(memory_space=pltpu.SMEM)] + [vmem] * len(blocks),
        out_specs=vmem,
        out_shape=jax.ShapeDtypeStruct((tokens, 2 * INNER * width), BF16),
        cost_estimate=pl.CostEstimate(flops=1, transcendentals=0, bytes_accessed=1),
        compiler_params=pltpu.CompilerParams(vmem_limit_bytes=16 * 2**20),
        name="place",
    )(flags, *blocks)


def pack_kernel(*refs):
    sources, out, sems = refs[:-2], refs[-2], refs[-1]
    copies, lane = [], 0
    for source in sources:
        width = source.shape[1]
        copies.append(pltpu.make_async_copy(
            source, out.at[:, lane : lane + width], sems.at[len(copies)]
        ))
        copies[-1].start()
        lane += width
    for copy in copies:
        copy.wait()


def pack(*sources):
    rows = sources[0].shape[0]
    depth = sum(source.shape[1] for source in sources)
    return pl.pallas_call(
        pack_kernel,
        in_specs=[pl.BlockSpec(memory_space=pltpu.HBM)] * len(sources),
        out_specs=pl.BlockSpec(memory_space=pltpu.VMEM),
        out_shape=jax.ShapeDtypeStruct((rows, depth), BF16),
        scratch_shapes=[pltpu.SemaphoreType.DMA((len(sources),))],
        compiler_params=pltpu.CompilerParams(vmem_limit_bytes=VMEM_LIMIT),
        cost_estimate=pl.CostEstimate(flops=1, transcendentals=0, bytes_accessed=1),
        name="pack",
    )(*sources)


def gate_kernel(*refs):
    pass


def gate(array, deps, flops=1):
    hbm = pl.BlockSpec(memory_space=pltpu.HBM)
    return pl.pallas_call(
        gate_kernel,
        in_specs=[hbm] * (1 + len(deps)),
        out_specs=hbm,
        out_shape=jax.ShapeDtypeStruct(array.shape, array.dtype),
        input_output_aliases={0: 0},
        compiler_params=pltpu.CompilerParams(vmem_limit_bytes=VMEM_LIMIT),
        cost_estimate=pl.CostEstimate(flops=flops, transcendentals=0, bytes_accessed=1),
        name="gate",
    )(array, *deps)


def join_kernel(dq, own, near, far, *refs):
    out = refs[-1]
    width = dq.shape[1]
    out[:, :width] = dq[...]
    out[:, width:] = (own[...] + near[...].astype(F32) + far[...].astype(F32)).astype(BF16)


def join(dq, own, near, far, deps):
    tokens, width = dq.shape
    vmem = pl.BlockSpec(memory_space=pltpu.VMEM)
    hbm = pl.BlockSpec(memory_space=pltpu.HBM)
    return pl.pallas_call(
        join_kernel,
        in_specs=[vmem] * 4 + [hbm] * len(deps),
        out_specs=vmem,
        out_shape=jax.ShapeDtypeStruct((tokens, width + own.shape[1]), BF16),
        compiler_params=pltpu.CompilerParams(vmem_limit_bytes=VMEM_LIMIT),
        cost_estimate=pl.CostEstimate(flops=2 * 10**9, transcendentals=0, bytes_accessed=1),
        name="join",
    )(dq, own, near, far, *deps)


def shifted(array, by):
    peers = lax.axis_size("seq")
    pairs = [(i, i + by) for i in range(peers) if 0 <= i + by < peers]
    return lax.ppermute(array, "seq", pairs)


def swapped(array, bits):
    peers = lax.axis_size("seq")
    return lax.ppermute(array, "seq", [(i, i ^ bits) for i in range(peers)])


def layered(array, moves):
    pairs = [(a * INNER + i, b * INNER + i) for a, b in moves for i in range(INNER)]
    return lax.ppermute(array, "seq", pairs)


def crossed(array, layers, inward):
    pairs = []
    for i in range(layers * INNER):
        half = i // INNER // (layers // 2)
        pairs.append((2 * i + 1 - half, 2 * i + half) if inward else (2 * i + half, 2 * i + 1 - half))
    return lax.ppermute(array, ("seq", "head"), pairs)


def returned(blocks):
    return [blocks[0], swapped(blocks[2], 1), swapped(blocks[1], 2), swapped(blocks[3], 3)]


def ordered(blocks, inner):
    cols = []
    for j in range(INNER):
        pick = blocks[j]
        for i in range(1, INNER):
            pick = jnp.where(inner == i, blocks[j ^ i], pick)
        cols.append(pick)
    return jnp.concatenate(cols, 1)


def project_gathered(grads, weight, layers, tokens, head, inner):
    rows = weight.shape[0]
    groups = [[z * INNER + i for z in range(layers)] for i in range(INNER)]
    every = lax.all_gather(weight, "seq", axis=0, tiled=True, axis_index_groups=groups)
    halves = every.reshape(2, layers // 2 * rows, -1)

    def times(piece):
        return lax.dot_general(
            grads, piece, (((1,), (1,)), ((), ())), preferred_element_type=F32
        )

    send = times(jnp.where(head == 0, halves[1], halves[0])).astype(BF16)
    got = lax.ppermute(send, "head", [(0, 1), (1, 0)])
    keep = times(jnp.where(head == 0, halves[0], halves[1]))
    blocks = returned((keep + got.astype(F32)).astype(BF16).reshape(INNER, tokens, -1))
    blocks = [b.reshape(tokens * (layers // 2), rows) for b in blocks]
    return ordered(blocks, inner).reshape(tokens, -1)


def tied(*arrays):
    return lax.optimization_barrier(arrays)


def shards(
    query, key, value, output, output_gradient, lse, doc_lengths, w_query, key_weight, value_weight
):
    tokens = query.shape[0]
    seq = lax.axis_index("seq")
    head = lax.axis_index("head")
    layer, inner = seq // INNER, seq % INNER
    layers = lax.axis_size("seq") // INNER
    half = layer // (layers // 2)
    line = layers == 4

    pair = pack(key, value)
    near = shifted(pair, 1)
    far = shifted(pair, 2)
    rows = w_query.shape[0]
    if line:
        weight = pack(w_query, key_weight, value_weight)
        mate = layered(weight, [(0, 1), (1, 0), (2, 3), (3, 2)])
        mid = layered(weight, [(1, 2), (2, 1)])
        third = layered(mid, [(1, 0), (2, 3)])
        fourth = layered(mate, [(1, 2), (2, 1)])
    else:
        weight = jnp.concatenate([w_query, key_weight, value_weight], 1)
    first = (seq * tokens).astype(jnp.int32).reshape(1)
    groups = key.shape[1] // HEAD_SIZE
    dq, earlier = [], []
    for g in range(groups):
        cost = (4 if g else 24) * 10**9
        dq_part, *parts = attention(
            g, cost, first, doc_lengths, query, output_gradient, output, lse,
            pair, near, far, earlier,
        )
        dq.append(dq_part)
        earlier += parts
    own_part, near_part, far_part = parts
    back_near = shifted(near_part, -1)
    back_far = shifted(far_part, -2)
    dq_y = [swapped(part, 2) for part in dq[:-1]]
    joined = join(dq[-1], own_part, back_near, back_far, [mate, mid, *dq_y] if line else [])
    joined_y = swapped(joined, 2)
    grads = [*dq[:-1], joined, *dq_y, joined_y]
    grads = grads + [swapped(g, 1) for g in grads]

    if not line:
        parts = len(grads) // INNER
        four = jnp.concatenate(
            [jnp.concatenate(grads[t * parts : (t + 1) * parts], 1) for t in range(INNER)], 0
        )
        return project_gathered(four, weight, layers, tokens, head, inner)

    weight = gate(weight, [third, fourth, joined_y])
    last = layered(weight, [(0, 3), (3, 0)])
    same = head == half
    send, held = project_send(layers, grads, weight, third, mid)
    got = lax.ppermute(send, "head", [(0, 1), (1, 0)])
    keep, mate_full, mate_low = project_keep(layers, held, weight, mate, third, mid, [send])
    got_mate = crossed(mate_low, layers, True)
    last_full, low_first, low_second = project_last(layers, held, last, fourth, [got])
    got_first = crossed(low_first, layers, False)
    got_second = crossed(low_second, layers, False)

    def lanes(array, k):
        return array[:, k * rows : (k + 1) * rows].astype(F32)

    sets = [returned([(keep[r] + lanes(got, r)).astype(BF16) for r in range(INNER)])]
    totals = []
    for r in range(INNER):
        got_last = lanes(got_first if r % 2 else got_second, r // 2)
        total = jnp.where(same, mate_full[r] + lanes(got_mate, r), last_full[r] + got_last)
        totals.append(total.astype(BF16))
    sets.append(returned(totals))
    a_first = jnp.where(same, layer % 2 == 0, half == 0)
    return place(jnp.stack([inner, a_first.astype(jnp.int32)]), sets)


def solution(mesh):
    in_specs = (
        P("seq", "head"),
        P("seq", "head"),
        P("seq", "head"),
        P("seq", "head"),
        P("seq", "head"),
        P("head", "seq"),
        P(),
        P("seq", "head"),
        P("seq", "head"),
        P("seq", "head"),
    )
    out_specs = P("seq", "head")
    return jax.shard_map(shards, mesh=mesh, in_specs=in_specs, out_specs=out_specs, check_vma=False)
```

```python
import functools
import math

import jax
import jax.numpy as jnp
from jax import lax
from jax.experimental import pallas as pl
from jax.experimental.pallas import tpu as pltpu
from jax.sharding import PartitionSpec as P

HEAD_SIZE = 128
WINDOW = 512
INNER = 4
LOG2E = 1.4426950408889634
VMEM_LIMIT = 63 * 2**20
JOIN_LIMIT = 63 * 2**20
F32 = jnp.float32
BF16 = jnp.bfloat16


def attention_kernel(
    group, groups, first_ref, docs_ref, q_ref, do_ref, o_ref, lse_ref,
    k_own_ref, v_own_ref, k_near_ref, v_near_ref, k_far_ref, v_far_ref,
    *refs,
):
    *earlier, dq_ref, own_ref, near_ref, far_ref, probs, dscores, do_rows, q_rows = refs
    tokens = k_own_ref.shape[0]
    per_group = q_ref.shape[1] // HEAD_SIZE
    scale = 1.0 / math.sqrt(HEAD_SIZE)
    rows = lax.broadcasted_iota(jnp.int32, (tokens, tokens), 0)
    cols = lax.broadcasted_iota(jnp.int32, (tokens, tokens), 1)
    causal = rows <= cols
    keep_own = jnp.where(causal, 1.0, 0.0).astype(BF16)
    first = first_ref[0]
    spot = first + lax.broadcasted_iota(jnp.int32, (8, tokens), 1)
    start = jnp.int32(0)
    doc_begin = jnp.zeros((8, tokens), jnp.int32)
    for d in range(docs_ref.shape[0]):
        doc_begin = jnp.maximum(doc_begin, jnp.where(start <= spot, start, 0))
        start = start + docs_ref[d]
    doc_row = doc_begin[0:1]
    mixed = first + rows - jnp.where(causal, 0, 2 * tokens)
    bias_mix = jnp.where(mixed >= doc_row, 0.0, -1e30)
    bias_near = jnp.where(first - tokens + rows >= doc_row, 0.0, -1e30)

    nt = (((1,), (1,)), ((), ()))
    tn = (((0,), (0,)), ((), ()))

    def dot(a, b, dims=(((1,), (0,)), ((), ()))):
        return lax.dot_general(a, b, dims, preferred_element_type=F32)

    keys = jnp.concatenate([k_own_ref[...], k_near_ref[...], k_far_ref[...]], 0)
    values = jnp.concatenate([v_own_ref[...], v_near_ref[...], v_far_ref[...]], 0)
    keys_t = keys.T
    own, near, far = slice(0, tokens), slice(tokens, 2 * tokens), slice(2 * tokens, 3 * tokens)
    def finish(j):
        span = slice(j * HEAD_SIZE, (j + 1) * HEAD_SIZE)
        turn = slice(j * tokens, (j + 1) * tokens)
        dq_ref[:, span] = dot(keys_t, dscores[:, turn]).T.astype(BF16)
        if j % 2:
            two = slice((j - 1) * tokens, (j + 1) * tokens)
        elif j == per_group - 1:
            two = turn
        else:
            return
        sums.append((dot(probs[:, two], do_rows[two, :]), dot(dscores[:, two], q_rows[two, :])))

    sums = []
    for j in range(per_group):
        span = slice(j * HEAD_SIZE, (j + 1) * HEAD_SIZE)
        turn = slice(j * tokens, (j + 1) * tokens)
        q, do, o = q_ref[:, span], do_ref[:, span], o_ref[:, span]
        q_rows[turn, :] = q
        do_rows[turn, :] = do
        head = group * per_group + j
        lse2 = lse_ref[head : head + 1, :] * LOG2E
        delta = jnp.sum((do.astype(F32) * o.astype(F32)).T, axis=0, keepdims=True)
        scores, grads = dot(keys, q, nt), dot(values, do, nt)

        if j:
            finish(j - 1)

        def both(score, grad, bias):
            prob = jnp.exp2(score * (scale * LOG2E) - lse2 + bias)
            return prob.astype(BF16), (prob * (grad - delta) * scale).astype(BF16)

        p_mix, ds_mix = both(
            jnp.where(causal, scores[own], scores[far]),
            jnp.where(causal, grads[own], grads[far]),
            bias_mix,
        )
        p_near, ds_near = both(scores[near], grads[near], bias_near)
        p_own, ds_own = p_mix * keep_own, ds_mix * keep_own
        probs[own, turn], probs[near, turn], probs[far, turn] = p_own, p_near, p_mix - p_own
        dscores[own, turn], dscores[near, turn], dscores[far, turn] = ds_own, ds_near, ds_mix - ds_own
    finish(per_group - 1)
    acc_v = functools.reduce(lambda a, b: a + b, [each[0] for each in sums])
    acc_k = functools.reduce(lambda a, b: a + b, [each[1] for each in sums])
    for i, ref in enumerate((own_ref, near_ref, far_ref)):
        part = slice(i * tokens, (i + 1) * tokens)
        if group < groups - 1:
            ref[:, :HEAD_SIZE] = acc_k[part].astype(ref.dtype)
            ref[:, HEAD_SIZE:] = acc_v[part].astype(ref.dtype)
            continue
        for g in range(groups):
            k_cols = slice(g * HEAD_SIZE, (g + 1) * HEAD_SIZE)
            v_cols = slice((groups + g) * HEAD_SIZE, (groups + g + 1) * HEAD_SIZE)
            if g == group:
                ref[:, k_cols] = acc_k[part].astype(ref.dtype)
                ref[:, v_cols] = acc_v[part].astype(ref.dtype)
            else:
                ref[:, k_cols] = earlier[3 * g + i][:, :HEAD_SIZE]
                ref[:, v_cols] = earlier[3 * g + i][:, HEAD_SIZE:]


def attention(group, cost, first, doc_lengths, query, output_gradient, output, lse, own, near, far, earlier):
    tokens, width = query.shape
    groups = own.shape[1] // (2 * HEAD_SIZE)
    kv_width = own.shape[1] if group == groups - 1 else 2 * HEAD_SIZE
    part = width // groups
    wide = pl.BlockSpec((tokens, part), lambda i: (0, group))
    per_group = part // HEAD_SIZE
    smem = pl.BlockSpec(memory_space=pltpu.SMEM)
    k_spec = pl.BlockSpec((tokens, HEAD_SIZE), lambda i: (0, group))
    v_spec = pl.BlockSpec((tokens, HEAD_SIZE), lambda i: (0, groups + group))

    def whole(shape):
        return pl.BlockSpec(shape, lambda i: (0, 0))

    return pl.pallas_call(
        functools.partial(attention_kernel, group, groups),
        grid=(1,),
        in_specs=[smem, smem, wide, wide, wide, whole(lse.shape)]
        + [k_spec, v_spec] * 3
        + [whole(array.shape) for array in earlier],
        out_specs=[whole((tokens, part))] + [whole((tokens, kv_width))] * 3,
        out_shape=[
            jax.ShapeDtypeStruct((tokens, part), BF16),
            jax.ShapeDtypeStruct((tokens, kv_width), F32),
            jax.ShapeDtypeStruct((tokens, kv_width), BF16),
            jax.ShapeDtypeStruct((tokens, kv_width), BF16),
        ],
        scratch_shapes=[
            pltpu.VMEM((3 * tokens, per_group * tokens), BF16),
            pltpu.VMEM((3 * tokens, per_group * tokens), BF16),
            pltpu.VMEM((per_group * tokens, HEAD_SIZE), BF16),
            pltpu.VMEM((per_group * tokens, HEAD_SIZE), BF16),
        ],
        compiler_params=pltpu.CompilerParams(vmem_limit_bytes=VMEM_LIMIT),
        cost_estimate=pl.CostEstimate(flops=cost, transcendentals=0, bytes_accessed=1),
        name="attention",
    )(
        first, doc_lengths, query, output_gradient, output, lse,
        own, own, near, near, far, far, *earlier,
    )


NT = (((1,), (1,)), ((), ()))


def grad_copies(grads, held, sems):
    parts = len(grads) // INNER
    tokens = grads[0].shape[0]
    copies = []
    for t in range(INNER):
        lane = 0
        copies.append([])
        for i, grad in enumerate(grads[t * parts : (t + 1) * parts]):
            width = grad.shape[1]
            copies[-1].append(pltpu.make_async_copy(
                grad,
                held.at[t * tokens : (t + 1) * tokens, lane : lane + width],
                sems.at[t * parts + i],
            ))
            lane += width
    for t in range(2):
        for copy in copies[t]:
            copy.start()

    def ready(t):
        for copy in copies[t]:
            copy.wait()
        if t + 2 < INNER:
            for copy in copies[t + 2]:
                copy.start()

    return ready


def standing(layers):
    layer = lax.axis_index("seq") // INNER
    at_edge = (layer == 0) | (layer == layers - 1)
    return at_edge, lax.axis_index("head") == layer // (layers // 2)


def fetch_either(choice, first, second, weight, sem):
    @pl.when(choice)
    def _():
        pltpu.make_async_copy(first, weight, sem).start()

    @pl.when(jnp.logical_not(choice))
    def _():
        pltpu.make_async_copy(second, weight, sem).start()


def times(grad, weight):
    return lax.dot_general(grad, weight, NT, preferred_element_type=F32)


def send_kernel(layers, count, *refs):
    grads, (own, edge, mid) = refs[:count], refs[count : count + 3]
    send, gathered, held, weight, sems = refs[-5:]
    tokens, cols = grads[0].shape[0], weight.shape[0]
    at_edge, same = standing(layers)

    @pl.when(same)
    def _():
        fetch_either(at_edge, edge, mid, weight, sems.at[count])

    @pl.when(jnp.logical_not(same))
    def _():
        pltpu.make_async_copy(own, weight, sems.at[count]).start()

    ready = grad_copies(grads, held, sems)
    pltpu.make_async_copy(own, weight, sems.at[count]).wait()
    stores = []
    for t in range(INNER):
        ready(t)
        rows = slice(t * tokens, (t + 1) * tokens)
        stores.append(pltpu.make_async_copy(
            held.at[rows], gathered.at[rows], sems.at[count + 1 + t]
        ))
        stores[-1].start()
        lanes = slice(t * cols, (t + 1) * cols)
        send[:, lanes] = times(held[rows, :], weight[...]).astype(BF16)
    for store in stores:
        store.wait()


def keep_kernel(layers, held, own, mate, edge, mid, *refs):
    keep, mate_full, mate_low, weights, sems = refs[-5:]
    cols = weights.shape[1]
    tokens = held.shape[0] // INNER
    at_edge, same = standing(layers)
    mate_copy = pltpu.make_async_copy(mate, weights.at[1], sems.at[1])
    mate_copy.start()

    @pl.when(same)
    def _():
        pltpu.make_async_copy(own, weights.at[0], sems.at[0]).start()

    @pl.when(jnp.logical_not(same))
    def _():
        fetch_either(at_edge, edge, mid, weights.at[0], sems.at[0])

    mate_copy.wait()
    for t in range(INNER):
        product = times(held[t * tokens : (t + 1) * tokens, :], weights[1])
        mate_full[t] = product
        mate_low[:, t * cols : (t + 1) * cols] = product.astype(BF16)
    pltpu.make_async_copy(own, weights.at[0], sems.at[0]).wait()
    for t in range(INNER):
        keep[t] = times(held[t * tokens : (t + 1) * tokens, :], weights[0])


def last_kernel(parts, layers, held, piece, passed, *refs):
    outs, weight, sem = refs[-2 - 2 * len(parts) : -2], refs[-2], refs[-1]
    at_edge, _ = standing(layers)
    fetch_either(at_edge, piece, passed, weight, sem)
    pltpu.make_async_copy(piece, weight, sem).wait()
    tokens, cols = held.shape[0] // INNER, weight.shape[0]
    for i, picks in enumerate(parts):
        full, low = outs[2 * i : 2 * i + 2]
        for k, t in enumerate(picks):
            product = times(held[t * tokens : (t + 1) * tokens, :], weight[...])
            full[k] = product
            low[:, k * cols : (k + 1) * cols] = product.astype(BF16)


def project(kernel, layers, operands, in_vmem, outs, scratch, limit, name):
    vmem = pl.BlockSpec(memory_space=pltpu.VMEM)
    hbm = pl.BlockSpec(memory_space=pltpu.HBM)
    return pl.pallas_call(
        functools.partial(kernel, layers),
        in_specs=[vmem] * in_vmem + [hbm] * (len(operands) - in_vmem),
        out_specs=[vmem if in_place else hbm for in_place, _, _ in outs],
        out_shape=[jax.ShapeDtypeStruct(shape, kind) for _, shape, kind in outs],
        scratch_shapes=scratch,
        compiler_params=pltpu.CompilerParams(vmem_limit_bytes=limit),
        cost_estimate=pl.CostEstimate(flops=1, transcendentals=0, bytes_accessed=1),
        name=name,
    )(*operands)


def project_send(layers, grads, own, edge, mid):
    tokens = grads[0].shape[0]
    cols, depth = own.shape
    return project(
        lambda layers, *refs: send_kernel(layers, len(grads), *refs),
        layers,
        [*grads, own, edge, mid],
        0,
        [(True, (tokens, INNER * cols), BF16), (False, (INNER * tokens, depth), BF16)],
        [
            pltpu.VMEM((INNER * tokens, depth), BF16),
            pltpu.VMEM((cols, depth), BF16),
            pltpu.SemaphoreType.DMA((len(grads) + 1 + INNER,)),
        ],
        VMEM_LIMIT,
        "project_send",
    )


def project_keep(layers, gathered, own, mate, edge, mid, after):
    tokens, depth = gathered.shape[0] // INNER, gathered.shape[1]
    cols = own.shape[0]
    full = (True, (INNER, tokens, cols), F32)
    return project(
        keep_kernel,
        layers,
        [gathered, own, mate, edge, mid, *after],
        1,
        [full, full, (True, (tokens, INNER * cols), BF16)],
        [pltpu.VMEM((2, cols, depth), BF16), pltpu.SemaphoreType.DMA((2,))],
        59 * 2**20,
        "project_keep",
    )


def project_last(parts, layers, gathered, piece, passed, after):
    tokens, cols = gathered.shape[0] // INNER, piece.shape[0]
    outs = []
    for picks in parts:
        outs.append((True, (len(picks), tokens, cols), F32))
        outs.append((True, (tokens, len(picks) * cols), BF16))
    return project(
        functools.partial(last_kernel, parts),
        layers,
        [gathered, piece, passed, *after],
        1,
        outs,
        [pltpu.VMEM(piece.shape, BF16), pltpu.SemaphoreType.DMA],
        10 * 2**20,
        "project_last",
    )


def combine_kernel(layers, picks, last_full, mate_full, got_mate, got_last, *refs):
    outs = refs[-len(picks) :]
    _, same = standing(layers)
    cols = last_full.shape[2]
    for k, r in enumerate(picks):
        @pl.when(same)
        def _():
            got = got_mate[:, r * cols : (r + 1) * cols].astype(F32)
            outs[k][...] = (mate_full[r] + got).astype(BF16)

        @pl.when(jnp.logical_not(same))
        def _():
            got = got_last[:, k * cols : (k + 1) * cols].astype(F32)
            outs[k][...] = (last_full[k] + got).astype(BF16)


def combine(layers, picks, last_full, mate_full, got_mate, got_last, after):
    _, tokens, cols = last_full.shape
    vmem = pl.BlockSpec(memory_space=pltpu.VMEM)
    return pl.pallas_call(
        functools.partial(combine_kernel, layers, picks),
        in_specs=[vmem] * 4 + [pl.BlockSpec(memory_space=pltpu.HBM)] * len(after),
        out_specs=[vmem] * len(picks),
        out_shape=[jax.ShapeDtypeStruct((tokens, cols), BF16)] * len(picks),
        compiler_params=pltpu.CompilerParams(vmem_limit_bytes=12 * 2**20),
        cost_estimate=pl.CostEstimate(flops=1, transcendentals=0, bytes_accessed=1),
        name="combine",
    )(last_full, mate_full, got_mate, got_last, *after)


def place_kernel(layers, tasks, *refs):
    out = refs[-1]
    width = refs[0].shape[1]
    if len(refs) > len(tasks) + 1:
        out[...] = refs[-2][...]
    seq = lax.axis_index("seq")
    layer, inner = seq // INNER, seq % INNER
    _, same = standing(layers)
    lower = layer // (layers // 2) == 0
    first_low = jnp.where(same, layer % 2 == 0, lower)
    for i in range(INNER):
        for low in (True, False):
            @pl.when((inner == i) & (first_low == low))
            def _():
                for block, (which, r) in zip(refs, tasks):
                    lane = ((which == 0) != low) * INNER * width + (r ^ i) * width
                    out[:, lane : lane + width] = block[...]


def place(layers, tasks, blocks, earlier, cost):
    tokens, width = blocks[0].shape
    vmem = pl.BlockSpec(memory_space=pltpu.VMEM)
    return pl.pallas_call(
        functools.partial(place_kernel, layers, tasks),
        in_specs=[vmem] * (len(blocks) + len(earlier)),
        out_specs=vmem,
        out_shape=jax.ShapeDtypeStruct((tokens, 2 * INNER * width), BF16),
        cost_estimate=pl.CostEstimate(flops=cost, transcendentals=0, bytes_accessed=1),
        compiler_params=pltpu.CompilerParams(vmem_limit_bytes=16 * 2**20),
        name="place",
    )(*blocks, *earlier)


def pack_kernel(splits, *refs):
    outs, sems = refs[-1 - len(splits) : -1], refs[-1]
    copies = []
    for out, (lo, hi) in zip(outs, splits):
        lane = 0
        for source in refs[lo:hi]:
            width = source.shape[1]
            copies.append(pltpu.make_async_copy(
                source, out.at[:, lane : lane + width], sems.at[len(copies)]
            ))
            copies[-1].start()
            lane += width
    for copy in copies:
        copy.wait()


def pack(*groups):
    sources, splits = [], []
    for group in groups:
        splits.append((len(sources), len(sources) + len(group)))
        sources += group
    return pl.pallas_call(
        functools.partial(pack_kernel, splits),
        in_specs=[pl.BlockSpec(memory_space=pltpu.HBM)] * len(sources),
        out_specs=[pl.BlockSpec(memory_space=pltpu.VMEM)] * len(groups),
        out_shape=[
            jax.ShapeDtypeStruct((g[0].shape[0], sum(each.shape[1] for each in g)), BF16)
            for g in groups
        ],
        scratch_shapes=[pltpu.SemaphoreType.DMA((len(sources),))],
        compiler_params=pltpu.CompilerParams(vmem_limit_bytes=VMEM_LIMIT),
        cost_estimate=pl.CostEstimate(flops=1, transcendentals=0, bytes_accessed=1),
        name="pack",
    )(*sources)


def gate_kernel(*refs):
    pass


def gate(array, deps, flops=1):
    hbm = pl.BlockSpec(memory_space=pltpu.HBM)
    return pl.pallas_call(
        gate_kernel,
        in_specs=[hbm] * (1 + len(deps)),
        out_specs=hbm,
        out_shape=jax.ShapeDtypeStruct(array.shape, array.dtype),
        input_output_aliases={0: 0},
        compiler_params=pltpu.CompilerParams(vmem_limit_bytes=VMEM_LIMIT),
        cost_estimate=pl.CostEstimate(flops=flops, transcendentals=0, bytes_accessed=1),
        name="gate",
    )(array, *deps)


def join_kernel(dq, own, near, far, *refs):
    out = refs[-1]
    width = dq.shape[1]
    out[:, :width] = dq[...]
    out[:, width:] = (own[...] + near[...].astype(F32) + far[...].astype(F32)).astype(BF16)


def join(dq, own, near, far, deps):
    tokens, width = dq.shape
    vmem = pl.BlockSpec(memory_space=pltpu.VMEM)
    hbm = pl.BlockSpec(memory_space=pltpu.HBM)
    return pl.pallas_call(
        join_kernel,
        in_specs=[vmem] * 4 + [hbm] * len(deps),
        out_specs=vmem,
        out_shape=jax.ShapeDtypeStruct((tokens, width + own.shape[1]), BF16),
        compiler_params=pltpu.CompilerParams(vmem_limit_bytes=JOIN_LIMIT),
        cost_estimate=pl.CostEstimate(flops=2 * 10**9, transcendentals=0, bytes_accessed=1),
        name="join",
    )(dq, own, near, far, *deps)


def shifted(array, by):
    peers = lax.axis_size("seq")
    pairs = [(i, i + by) for i in range(peers) if 0 <= i + by < peers]
    return lax.ppermute(array, "seq", pairs)


def swapped(array, bits):
    peers = lax.axis_size("seq")
    return lax.ppermute(array, "seq", [(i, i ^ bits) for i in range(peers)])


def layered(array, moves):
    pairs = [(a * INNER + i, b * INNER + i) for a, b in moves for i in range(INNER)]
    return lax.ppermute(array, "seq", pairs)


def crossed(array, layers, inward):
    pairs = []
    for i in range(layers * INNER):
        half = i // INNER // (layers // 2)
        pairs.append((2 * i + 1 - half, 2 * i + half) if inward else (2 * i + half, 2 * i + 1 - half))
    return lax.ppermute(array, ("seq", "head"), pairs)


def returned(blocks):
    return [blocks[0], swapped(blocks[2], 1), swapped(blocks[1], 2), swapped(blocks[3], 3)]


def ordered(blocks, inner):
    cols = []
    for j in range(INNER):
        pick = blocks[j]
        for i in range(1, INNER):
            pick = jnp.where(inner == i, blocks[j ^ i], pick)
        cols.append(pick)
    return jnp.concatenate(cols, 1)


def project_gathered(grads, weight, layers, tokens, head, inner):
    rows = weight.shape[0]
    groups = [[z * INNER + i for z in range(layers)] for i in range(INNER)]
    every = lax.all_gather(weight, "seq", axis=0, tiled=True, axis_index_groups=groups)
    halves = every.reshape(2, layers // 2 * rows, -1)

    def times(piece):
        return lax.dot_general(
            grads, piece, (((1,), (1,)), ((), ())), preferred_element_type=F32
        )

    send = times(jnp.where(head == 0, halves[1], halves[0])).astype(BF16)
    got = lax.ppermute(send, "head", [(0, 1), (1, 0)])
    keep = times(jnp.where(head == 0, halves[0], halves[1]))
    blocks = returned((keep + got.astype(F32)).astype(BF16).reshape(INNER, tokens, -1))
    blocks = [b.reshape(tokens * (layers // 2), rows) for b in blocks]
    return ordered(blocks, inner).reshape(tokens, -1)


def tied(*arrays):
    return lax.optimization_barrier(arrays)


def shards(
    query, key, value, output, output_gradient, lse, doc_lengths, w_query, key_weight, value_weight
):
    tokens = query.shape[0]
    seq = lax.axis_index("seq")
    head = lax.axis_index("head")
    inner = seq % INNER
    layers = lax.axis_size("seq") // INNER
    line = layers == 4

    rows = w_query.shape[0]
    if line:
        pair, weight = pack((key, value), (w_query, key_weight, value_weight))
    else:
        pair = jnp.concatenate([key, value], 1)
        weight = jnp.concatenate([w_query, key_weight, value_weight], 1)
    pair_width = pair.shape[1]
    near = shifted(pair, 1)
    far = shifted(pair, 2)
    if line:
        mate = layered(weight, [(0, 1), (1, 0), (2, 3), (3, 2)])
        mid = layered(weight, [(1, 2), (2, 1)])
        third = layered(mid, [(1, 0), (2, 3)])
        fourth = layered(mate, [(1, 2), (2, 1)])
    first = (seq * tokens).astype(jnp.int32).reshape(1)
    groups = key.shape[1] // HEAD_SIZE
    dq, earlier = [], []
    for g in range(groups):
        dq_part, *parts = attention(
            g, (4 if g else 24) * 10**9, first, doc_lengths, query, output_gradient, output, lse,
            pair, near, far, earlier,
        )
        dq.append(dq_part)
        earlier += parts
    own_part, near_part, far_part = parts
    dq_y = [swapped(part, 2) for part in dq[:-1]]
    back_near = shifted(near_part, -1)
    back_far = shifted(far_part, -2)
    deps = [mate, mid, *dq_y] if line else []
    joined = join(dq[-1], own_part, back_near, back_far, deps)
    joined_y = swapped(joined, 2)
    grads = [*dq[:-1], joined, *dq_y, joined_y]
    others = [swapped(g, 1) for g in grads]
    grads = grads + others

    if not line:
        parts = len(grads) // INNER
        four = jnp.concatenate(
            [jnp.concatenate(grads[t * parts : (t + 1) * parts], 1) for t in range(INNER)], 0
        )
        return project_gathered(four, weight, layers, tokens, head, inner)

    early = [o for o, g in zip(others, grads) if g is not joined and g is not joined_y]
    weight = gate(weight, [third, fourth, joined_y, *early])
    last = layered(weight, [(0, 3), (3, 0)])
    send, held = project_send(layers, grads, weight, third, mid)
    got = lax.ppermute(send, "head", [(0, 1), (1, 0)])
    keep, mate_full, mate_low = project_keep(layers, held, weight, mate, third, mid, [send])
    got_mate = crossed(mate_low, layers, True)
    parts = ((1, 3), (0, 2))
    outs = project_last(parts, layers, held, last, fourth, [got])
    halves = [
        (picks, outs[2 * i], crossed(outs[2 * i + 1], layers, False))
        for i, picks in enumerate(parts)
    ]

    def lanes(array, k):
        return array[:, k * rows : (k + 1) * rows].astype(F32)

    sets = [returned([(keep[r] + lanes(got, r)).astype(BF16) for r in range(INNER)])]
    blocks, after = [None] * INNER, sets[0][1:]
    for picks, full, got_last in halves:
        after = combine(layers, picks, full, mate_full, got_mate, got_last, after)
        for r, block in zip(picks, after):
            blocks[r] = block
    sets.append(returned(blocks))
    tasks = [*((0, r) for r in range(INNER)), (1, 2), (1, 3), (1, 0), (1, 1)]
    blocks = [sets[which][r] for which, r in tasks]
    partly = place(layers, tasks[:-2], blocks[:-2], [], 4 * 10**9)
    return place(layers, tasks[-2:], blocks[-2:], [partly], 1)


def solution(mesh):
    in_specs = (
        P("seq", "head"),
        P("seq", "head"),
        P("seq", "head"),
        P("seq", "head"),
        P("seq", "head"),
        P("head", "seq"),
        P(),
        P("seq", "head"),
        P("seq", "head"),
        P("seq", "head"),
    )
    out_specs = P("seq", "head")
    return jax.shard_map(shards, mesh=mesh, in_specs=in_specs, out_specs=out_specs, check_vma=False)
```

```python
import functools
import math

import jax
import jax.numpy as jnp
from jax import lax
from jax.experimental import pallas as pl
from jax.experimental.pallas import tpu as pltpu
from jax.sharding import PartitionSpec as P

HEAD_SIZE = 128
WINDOW = 512
INNER = 4
LOG2E = 1.4426950408889634
VMEM_LIMIT = 63 * 2**20
JOIN_COST = 10**9 + 1
ATTENTION_COST = 9 * 10**8
F32 = jnp.float32
BF16 = jnp.bfloat16


def attention_kernel(
    group, groups, first_ref, docs_ref, q_ref, do_ref, o_ref, lse_ref,
    k_own_ref, v_own_ref, k_near_ref, v_near_ref, k_far_ref, v_far_ref,
    *refs,
):
    *earlier, dq_ref, own_ref, near_ref, far_ref, probs, dscores, do_rows, q_rows = refs
    tokens = k_own_ref.shape[0]
    per_group = q_ref.shape[1] // HEAD_SIZE
    scale = 1.0 / math.sqrt(HEAD_SIZE)
    rows = lax.broadcasted_iota(jnp.int32, (tokens, tokens), 0)
    cols = lax.broadcasted_iota(jnp.int32, (tokens, tokens), 1)
    causal = rows <= cols
    keep_own = jnp.where(causal, 1.0, 0.0).astype(BF16)
    first = first_ref[0]
    spot = first + lax.broadcasted_iota(jnp.int32, (8, tokens), 1)
    start = jnp.int32(0)
    doc_begin = jnp.zeros((8, tokens), jnp.int32)
    for d in range(docs_ref.shape[0]):
        doc_begin = jnp.maximum(doc_begin, jnp.where(start <= spot, start, 0))
        start = start + docs_ref[d]
    doc_row = doc_begin[0:1]
    mixed = first + rows - jnp.where(causal, 0, 2 * tokens)
    bias_mix = jnp.where(mixed >= doc_row, 0.0, -1e30)
    bias_near = jnp.where(first - tokens + rows >= doc_row, 0.0, -1e30)

    nt = (((1,), (1,)), ((), ()))
    tn = (((0,), (0,)), ((), ()))

    def dot(a, b, dims=(((1,), (0,)), ((), ()))):
        return lax.dot_general(a, b, dims, preferred_element_type=F32)

    keys = jnp.concatenate([k_own_ref[...], k_near_ref[...], k_far_ref[...]], 0)
    values = jnp.concatenate([v_own_ref[...], v_near_ref[...], v_far_ref[...]], 0)
    keys_t = keys.T
    own, near, far = slice(0, tokens), slice(tokens, 2 * tokens), slice(2 * tokens, 3 * tokens)
    def finish(j):
        span = slice(j * HEAD_SIZE, (j + 1) * HEAD_SIZE)
        turn = slice(j * tokens, (j + 1) * tokens)
        dq_ref[:, span] = dot(keys_t, dscores[:, turn]).T.astype(BF16)
        if j % 2:
            two = slice((j - 1) * tokens, (j + 1) * tokens)
        elif j == per_group - 1:
            two = turn
        else:
            return
        sums.append((dot(probs[:, two], do_rows[two, :]), dot(dscores[:, two], q_rows[two, :])))

    sums = []
    for j in range(per_group):
        span = slice(j * HEAD_SIZE, (j + 1) * HEAD_SIZE)
        turn = slice(j * tokens, (j + 1) * tokens)
        q, do, o = q_ref[:, span], do_ref[:, span], o_ref[:, span]
        q_rows[turn, :] = q
        do_rows[turn, :] = do
        head = group * per_group + j
        lse2 = lse_ref[head : head + 1, :] * LOG2E
        delta = jnp.sum((do.astype(F32) * o.astype(F32)).T, axis=0, keepdims=True)
        scores, grads = dot(keys, q, nt), dot(values, do, nt)

        if j:
            finish(j - 1)

        def both(score, grad, bias):
            prob = jnp.exp2(score * (scale * LOG2E) - lse2 + bias)
            return prob.astype(BF16), (prob * (grad - delta) * scale).astype(BF16)

        p_mix, ds_mix = both(
            jnp.where(causal, scores[own], scores[far]),
            jnp.where(causal, grads[own], grads[far]),
            bias_mix,
        )
        p_near, ds_near = both(scores[near], grads[near], bias_near)
        p_own, ds_own = p_mix * keep_own, ds_mix * keep_own
        probs[own, turn], probs[near, turn], probs[far, turn] = p_own, p_near, p_mix - p_own
        dscores[own, turn], dscores[near, turn], dscores[far, turn] = ds_own, ds_near, ds_mix - ds_own
    finish(per_group - 1)
    acc_v = functools.reduce(lambda a, b: a + b, [each[0] for each in sums])
    acc_k = functools.reduce(lambda a, b: a + b, [each[1] for each in sums])
    for i, ref in enumerate((own_ref, near_ref, far_ref)):
        part = slice(i * tokens, (i + 1) * tokens)
        if group < groups - 1:
            ref[:, :HEAD_SIZE] = acc_k[part].astype(ref.dtype)
            ref[:, HEAD_SIZE:] = acc_v[part].astype(ref.dtype)
            continue
        for g in range(groups):
            k_cols = slice(g * HEAD_SIZE, (g + 1) * HEAD_SIZE)
            v_cols = slice((groups + g) * HEAD_SIZE, (groups + g + 1) * HEAD_SIZE)
            if g == group:
                ref[:, k_cols] = acc_k[part].astype(ref.dtype)
                ref[:, v_cols] = acc_v[part].astype(ref.dtype)
            else:
                ref[:, k_cols] = earlier[3 * g + i][:, :HEAD_SIZE]
                ref[:, v_cols] = earlier[3 * g + i][:, HEAD_SIZE:]


def attention(group, cost, first, doc_lengths, query, output_gradient, output, lse, own, near, far, earlier):
    tokens, width = query.shape
    groups = own.shape[1] // (2 * HEAD_SIZE)
    kv_width = own.shape[1] if group == groups - 1 else 2 * HEAD_SIZE
    part = width // groups
    wide = pl.BlockSpec((tokens, part), lambda i: (0, group))
    per_group = part // HEAD_SIZE
    smem = pl.BlockSpec(memory_space=pltpu.SMEM)
    k_spec = pl.BlockSpec((tokens, HEAD_SIZE), lambda i: (0, group))
    v_spec = pl.BlockSpec((tokens, HEAD_SIZE), lambda i: (0, groups + group))

    def whole(shape):
        return pl.BlockSpec(shape, lambda i: (0, 0))

    return pl.pallas_call(
        functools.partial(attention_kernel, group, groups),
        grid=(1,),
        in_specs=[smem, smem, wide, wide, wide, whole(lse.shape)]
        + [k_spec, v_spec] * 3
        + [whole(array.shape) for array in earlier],
        out_specs=[whole((tokens, part))] + [whole((tokens, kv_width))] * 3,
        out_shape=[
            jax.ShapeDtypeStruct((tokens, part), BF16),
            jax.ShapeDtypeStruct((tokens, kv_width), F32),
            jax.ShapeDtypeStruct((tokens, kv_width), BF16),
            jax.ShapeDtypeStruct((tokens, kv_width), BF16),
        ],
        scratch_shapes=[
            pltpu.VMEM((3 * tokens, per_group * tokens), BF16),
            pltpu.VMEM((3 * tokens, per_group * tokens), BF16),
            pltpu.VMEM((per_group * tokens, HEAD_SIZE), BF16),
            pltpu.VMEM((per_group * tokens, HEAD_SIZE), BF16),
        ],
        compiler_params=pltpu.CompilerParams(vmem_limit_bytes=VMEM_LIMIT),
        cost_estimate=pl.CostEstimate(flops=cost, transcendentals=0, bytes_accessed=1),
        name="attention",
    )(
        first, doc_lengths, query, output_gradient, output, lse,
        own, own, near, near, far, far, *earlier,
    )


NT = (((1,), (1,)), ((), ()))


def grad_copies(grads, held, sems):
    parts = len(grads) // INNER
    tokens = grads[0].shape[0]
    copies = []
    for t in range(INNER):
        lane = 0
        copies.append([])
        for i, grad in enumerate(grads[t * parts : (t + 1) * parts]):
            width = grad.shape[1]
            copies[-1].append(pltpu.make_async_copy(
                grad,
                held.at[t * tokens : (t + 1) * tokens, lane : lane + width],
                sems.at[t * parts + i],
            ))
            lane += width
    for t in range(2):
        for copy in copies[t]:
            copy.start()

    def ready(t):
        for copy in copies[t]:
            copy.wait()
        if t + 2 < INNER:
            for copy in copies[t + 2]:
                copy.start()

    return ready


def standing(layers):
    layer = lax.axis_index("seq") // INNER
    return lax.axis_index("head") == layer // (layers // 2)


def fetch_by_layer(sources, weight, sem):
    layer = lax.axis_index("seq") // INNER
    for z, source in enumerate(sources):
        @pl.when(layer == z)
        def _():
            pltpu.make_async_copy(source, weight, sem).start()


def times(grad, weight):
    return lax.dot_general(grad, weight, NT, preferred_element_type=F32)


def send_kernel(layers, count, *refs):
    grads, (own, *third) = refs[:count], refs[count : count + 1 + layers]
    send, gathered, held, weight, sems = refs[-5:]
    tokens, cols = grads[0].shape[0], weight.shape[0]
    same = standing(layers)

    @pl.when(same)
    def _():
        fetch_by_layer(third, weight, sems.at[count])

    @pl.when(jnp.logical_not(same))
    def _():
        pltpu.make_async_copy(own, weight, sems.at[count]).start()

    ready = grad_copies(grads, held, sems)
    pltpu.make_async_copy(own, weight, sems.at[count]).wait()
    stores = []
    for t in range(INNER):
        ready(t)
        rows = slice(t * tokens, (t + 1) * tokens)
        stores.append(pltpu.make_async_copy(
            held.at[rows], gathered.at[rows], sems.at[count + 1 + t]
        ))
        stores[-1].start()
        lanes = slice(t * cols, (t + 1) * cols)
        send[:, lanes] = times(held[rows, :], weight[...]).astype(BF16)
    for store in stores:
        store.wait()


def keep_kernel(layers, held, own, *refs):
    mate, third = refs[:layers], refs[layers : 2 * layers]
    keep, mate_full, mate_low, weights, sems = refs[-5:]
    cols = weights.shape[1]
    tokens = held.shape[0] // INNER
    same = standing(layers)
    fetch_by_layer(mate, weights.at[1], sems.at[1])

    @pl.when(same)
    def _():
        pltpu.make_async_copy(own, weights.at[0], sems.at[0]).start()

    @pl.when(jnp.logical_not(same))
    def _():
        fetch_by_layer(third, weights.at[0], sems.at[0])

    pltpu.make_async_copy(own, weights.at[1], sems.at[1]).wait()
    for t in range(INNER):
        product = times(held[t * tokens : (t + 1) * tokens, :], weights[1])
        mate_full[t] = product
        mate_low[:, t * cols : (t + 1) * cols] = product.astype(BF16)
    pltpu.make_async_copy(own, weights.at[0], sems.at[0]).wait()
    for t in range(INNER):
        keep[t] = times(held[t * tokens : (t + 1) * tokens, :], weights[0])


def last_kernel(order, layers, held, *refs):
    full, first, second, weight, sem = refs[-5:]
    fetch_by_layer(refs[:layers], weight, sem)
    pltpu.make_async_copy(refs[0], weight, sem).wait()
    tokens, cols = held.shape[0] // INNER, weight.shape[0]
    edge = first.shape[1]
    for k, t in enumerate(order):
        product = times(held[t * tokens : (t + 1) * tokens, :], weight[...])
        full[t] = product
        low = product.astype(BF16)
        lo, hi = k * cols, (k + 1) * cols
        if lo < edge:
            first[:, lo : min(hi, edge)] = low[:, : min(hi, edge) - lo]
        if hi > edge:
            second[:, max(lo, edge) - edge : hi - edge] = low[:, max(lo, edge) - lo :]


def project(kernel, layers, operands, in_vmem, outs, scratch, limit, name):
    vmem = pl.BlockSpec(memory_space=pltpu.VMEM)
    hbm = pl.BlockSpec(memory_space=pltpu.HBM)
    return pl.pallas_call(
        functools.partial(kernel, layers),
        in_specs=[vmem] * in_vmem + [hbm] * (len(operands) - in_vmem),
        out_specs=[vmem if in_place else hbm for in_place, _, _ in outs],
        out_shape=[jax.ShapeDtypeStruct(shape, kind) for _, shape, kind in outs],
        scratch_shapes=scratch,
        compiler_params=pltpu.CompilerParams(vmem_limit_bytes=limit),
        cost_estimate=pl.CostEstimate(flops=1, transcendentals=0, bytes_accessed=1),
        name=name,
    )(*operands)


def project_send(layers, grads, own, third):
    tokens = grads[0].shape[0]
    cols, depth = own.shape
    return project(
        lambda layers, *refs: send_kernel(layers, len(grads), *refs),
        layers,
        [*grads, own, *third],
        0,
        [(True, (tokens, INNER * cols), BF16), (False, (INNER * tokens, depth), BF16)],
        [
            pltpu.VMEM((INNER * tokens, depth), BF16),
            pltpu.VMEM((cols, depth), BF16),
            pltpu.SemaphoreType.DMA((len(grads) + 1 + INNER,)),
        ],
        VMEM_LIMIT,
        "project_send",
    )


def project_keep(layers, gathered, own, mate, third, after):
    tokens, depth = gathered.shape[0] // INNER, gathered.shape[1]
    cols = own.shape[0]
    full = (True, (INNER, tokens, cols), F32)
    return project(
        keep_kernel,
        layers,
        [gathered, own, *mate, *third, *after],
        1,
        [full, full, (True, (tokens, INNER * cols), BF16)],
        [pltpu.VMEM((2, cols, depth), BF16), pltpu.SemaphoreType.DMA((2,))],
        59 * 2**20,
        "project_keep",
    )


def project_last(order, layers, gathered, late, after):
    tokens, cols = gathered.shape[0] // INNER, late[0].shape[0]
    edge = -(-INNER // 2 * cols // HEAD_SIZE) * HEAD_SIZE
    return project(
        functools.partial(last_kernel, order),
        layers,
        [gathered, *late, *after],
        1,
        [
            (True, (INNER, tokens, cols), F32),
            (True, (tokens, edge), BF16),
            (True, (tokens, INNER * cols - edge), BF16),
        ],
        [pltpu.VMEM(late[0].shape, BF16), pltpu.SemaphoreType.DMA],
        10 * 2**20,
        "project_last",
    )


def combine_kernel(layers, order, picks, count, last_full, mate_full, got_mate, *refs):
    gots, outs = refs[:count], refs[-len(picks) :]
    same = standing(layers)
    cols = last_full.shape[2]
    for out, r in zip(outs, picks):
        @pl.when(same)
        def _():
            got = got_mate[:, r * cols : (r + 1) * cols].astype(F32)
            out[...] = (mate_full[r] + got).astype(BF16)

        @pl.when(jnp.logical_not(same))
        def _():
            start, begin = order.index(r) * cols, 0
            for got in gots:
                lo, hi = max(start, begin), min(start + cols, begin + got.shape[1])
                if lo < hi:
                    part = got[:, lo - begin : hi - begin].astype(F32)
                    total = last_full[r, :, lo - start : hi - start] + part
                    out[:, lo - start : hi - start] = total.astype(BF16)
                begin += got.shape[1]


def combine(layers, order, picks, last_full, mate_full, got_mate, gots, after):
    _, tokens, cols = last_full.shape
    vmem = pl.BlockSpec(memory_space=pltpu.VMEM)
    return pl.pallas_call(
        functools.partial(combine_kernel, layers, order, picks, len(gots)),
        in_specs=[vmem] * (3 + len(gots)) + [pl.BlockSpec(memory_space=pltpu.HBM)] * len(after),
        out_specs=[vmem] * len(picks),
        out_shape=[jax.ShapeDtypeStruct((tokens, cols), BF16)] * len(picks),
        compiler_params=pltpu.CompilerParams(vmem_limit_bytes=12 * 2**20),
        cost_estimate=pl.CostEstimate(flops=1, transcendentals=0, bytes_accessed=1),
        name="combine",
    )(last_full, mate_full, got_mate, *gots, *after)


def place_kernel(layers, tasks, *refs):
    out = refs[-1]
    width = refs[0].shape[1]
    if len(refs) > len(tasks) + 1:
        out[...] = refs[-2][...]
    seq = lax.axis_index("seq")
    layer, inner = seq // INNER, seq % INNER
    same = standing(layers)
    lower = layer // (layers // 2) == 0
    first_low = jnp.where(same, layer % 2 == 0, lower)
    for i in range(INNER):
        for low in (True, False):
            @pl.when((inner == i) & (first_low == low))
            def _():
                for block, (which, r) in zip(refs, tasks):
                    lane = ((which == 0) != low) * INNER * width + (r ^ i) * width
                    out[:, lane : lane + width] = block[...]


def place(layers, tasks, blocks, earlier, cost):
    tokens, width = blocks[0].shape
    vmem = pl.BlockSpec(memory_space=pltpu.VMEM)
    return pl.pallas_call(
        functools.partial(place_kernel, layers, tasks),
        in_specs=[vmem] * (len(blocks) + len(earlier)),
        out_specs=vmem,
        out_shape=jax.ShapeDtypeStruct((tokens, 2 * INNER * width), BF16),
        cost_estimate=pl.CostEstimate(flops=cost, transcendentals=0, bytes_accessed=1),
        compiler_params=pltpu.CompilerParams(vmem_limit_bytes=16 * 2**20),
        name="place",
    )(*blocks, *earlier)


def pack_kernel(splits, *refs):
    outs, sems = refs[-1 - len(splits) : -1], refs[-1]
    copies = []
    for out, (lo, hi) in zip(outs, splits):
        lane = 0
        for source in refs[lo:hi]:
            width = source.shape[1]
            copies.append(pltpu.make_async_copy(
                source, out.at[:, lane : lane + width], sems.at[len(copies)]
            ))
            copies[-1].start()
            lane += width
    for copy in copies:
        copy.wait()


def pack(*groups):
    sources, splits = [], []
    for group in groups:
        splits.append((len(sources), len(sources) + len(group)))
        sources += group
    return pl.pallas_call(
        functools.partial(pack_kernel, splits),
        in_specs=[pl.BlockSpec(memory_space=pltpu.HBM)] * len(sources),
        out_specs=[pl.BlockSpec(memory_space=pltpu.VMEM)] * len(groups),
        out_shape=[
            jax.ShapeDtypeStruct((g[0].shape[0], sum(each.shape[1] for each in g)), BF16)
            for g in groups
        ],
        scratch_shapes=[pltpu.SemaphoreType.DMA((len(sources),))],
        compiler_params=pltpu.CompilerParams(vmem_limit_bytes=VMEM_LIMIT),
        cost_estimate=pl.CostEstimate(flops=1, transcendentals=0, bytes_accessed=1),
        name="pack",
    )(*sources)


def gate_kernel(*refs):
    pass


def gate(array, deps, flops=1):
    hbm = pl.BlockSpec(memory_space=pltpu.HBM)
    return pl.pallas_call(
        gate_kernel,
        in_specs=[hbm] * (1 + len(deps)),
        out_specs=hbm,
        out_shape=jax.ShapeDtypeStruct(array.shape, array.dtype),
        input_output_aliases={0: 0},
        compiler_params=pltpu.CompilerParams(vmem_limit_bytes=VMEM_LIMIT),
        cost_estimate=pl.CostEstimate(flops=flops, transcendentals=0, bytes_accessed=1),
        name="gate",
    )(array, *deps)


def is_odd():
    return lax.axis_index("seq") % 2 == 1


def choose_kernel(odd_ref, even_ref, out):
    @pl.when(is_odd())
    def _():
        out[...] = odd_ref[...]

    @pl.when(jnp.logical_not(is_odd()))
    def _():
        out[...] = even_ref[...]


def merge_kernel(far, got, *refs):
    out = refs[-1]
    out[...] = far[...]

    @pl.when(is_odd())
    def _():
        out[...] = (far[...].astype(F32) + got[...].astype(F32)).astype(BF16)


def join_kernel(dq, own, got, back, *refs):
    out = refs[-1]
    width = dq.shape[1]
    out[:, :width] = dq[...]
    total = own[...] + back[...].astype(F32)

    @pl.when(is_odd())
    def _():
        out[:, width:] = total.astype(BF16)

    @pl.when(jnp.logical_not(is_odd()))
    def _():
        out[:, width:] = (total + got[...].astype(F32)).astype(BF16)


def small(kernel, arrays, deps, width, name, limit=6 * 2**20, cost=1):
    vmem = pl.BlockSpec(memory_space=pltpu.VMEM)
    hbm = pl.BlockSpec(memory_space=pltpu.HBM)
    return pl.pallas_call(
        kernel,
        in_specs=[vmem] * len(arrays) + [hbm] * len(deps),
        out_specs=vmem,
        out_shape=jax.ShapeDtypeStruct((arrays[0].shape[0], width), BF16),
        compiler_params=pltpu.CompilerParams(vmem_limit_bytes=limit),
        cost_estimate=pl.CostEstimate(flops=cost, transcendentals=0, bytes_accessed=1),
        name=name,
    )(*arrays, *deps)


def shifted(array, by):
    peers = lax.axis_size("seq")
    pairs = [(i, i + by) for i in range(peers) if 0 <= i + by < peers]
    return lax.ppermute(array, "seq", pairs)


def swapped(array, bits):
    peers = lax.axis_size("seq")
    return lax.ppermute(array, "seq", [(i, i ^ bits) for i in range(peers)])


def layered(array, moves):
    pairs = [(a * INNER + i, b * INNER + i) for a, b in moves for i in range(INNER)]
    return lax.ppermute(array, "seq", pairs)


def crossed(array, layers, inward):
    pairs = []
    for i in range(layers * INNER):
        half = i // INNER // (layers // 2)
        pairs.append((2 * i + 1 - half, 2 * i + half) if inward else (2 * i + half, 2 * i + 1 - half))
    return lax.ppermute(array, ("seq", "head"), pairs)


def returned(blocks):
    return [blocks[0], swapped(blocks[2], 1), swapped(blocks[1], 2), swapped(blocks[3], 3)]


def ordered(blocks, inner):
    cols = []
    for j in range(INNER):
        pick = blocks[j]
        for i in range(1, INNER):
            pick = jnp.where(inner == i, blocks[j ^ i], pick)
        cols.append(pick)
    return jnp.concatenate(cols, 1)


def project_gathered(grads, weight, layers, tokens, head, inner):
    rows = weight.shape[0]
    groups = [[z * INNER + i for z in range(layers)] for i in range(INNER)]
    every = lax.all_gather(weight, "seq", axis=0, tiled=True, axis_index_groups=groups)
    halves = every.reshape(2, layers // 2 * rows, -1)

    def times(piece):
        return lax.dot_general(
            grads, piece, (((1,), (1,)), ((), ())), preferred_element_type=F32
        )

    send = times(jnp.where(head == 0, halves[1], halves[0])).astype(BF16)
    got = lax.ppermute(send, "head", [(0, 1), (1, 0)])
    keep = times(jnp.where(head == 0, halves[0], halves[1]))
    blocks = returned((keep + got.astype(F32)).astype(BF16).reshape(INNER, tokens, -1))
    blocks = [b.reshape(tokens * (layers // 2), rows) for b in blocks]
    return ordered(blocks, inner).reshape(tokens, -1)


def tied(*arrays):
    return lax.optimization_barrier(arrays)


def shards(
    query, key, value, output, output_gradient, lse, doc_lengths, w_query, key_weight, value_weight
):
    tokens = query.shape[0]
    seq = lax.axis_index("seq")
    head = lax.axis_index("head")
    inner = seq % INNER
    layers = lax.axis_size("seq") // INNER
    line = layers == 4

    rows = w_query.shape[0]
    if line:
        pair, weight = pack((key, value), (w_query, key_weight, value_weight))
    else:
        pair = jnp.concatenate([key, value], 1)
        weight = jnp.concatenate([w_query, key_weight, value_weight], 1)
    pair_width = pair.shape[1]
    far = shifted(pair, 2)
    near = swapped(small(choose_kernel, [far, pair], [], pair.shape[1], "choose"), 1)
    if line:
        up = layered(weight, [(0, 1), (1, 2), (2, 3)])
        down = layered(weight, [(1, 0), (2, 1), (3, 2)])
    first = (seq * tokens).astype(jnp.int32).reshape(1)
    groups = key.shape[1] // HEAD_SIZE
    dq, earlier = [], []
    for g in range(groups):
        dq_part, *parts = attention(
            g, ATTENTION_COST, first, doc_lengths, query, output_gradient, output, lse,
            pair, near, far, earlier,
        )
        dq.append(dq_part)
        earlier += parts
    own_part, near_part, far_part = parts
    dq_y = [swapped(part, 2) for part in dq[:-1]]
    if line:
        down = gate(down, dq_y)
        up_on = layered(up, [(1, 2), (2, 3)])
        down_on = layered(down, [(1, 0), (2, 1)])
    got = swapped(near_part, 1)
    back = shifted(small(merge_kernel, [far_part, got], [], pair.shape[1], "merge"), -2)
    deps = [up, down] if line else []
    width = dq[-1].shape[1] + pair.shape[1]
    joined = small(
        join_kernel, [dq[-1], own_part, got, back], deps, width, "join", VMEM_LIMIT, JOIN_COST
    )
    joined_y = swapped(joined, 2)
    grads = [*dq[:-1], joined, *dq_y, joined_y]
    others = [swapped(g, 1) for g in grads]
    grads = grads + others

    if not line:
        parts = len(grads) // INNER
        four = jnp.concatenate(
            [jnp.concatenate(grads[t * parts : (t + 1) * parts], 1) for t in range(INNER)], 0
        )
        return project_gathered(four, weight, layers, tokens, head, inner)

    early = [o for o, g in zip(others, grads) if g is not joined and g is not joined_y]
    weight = gate(weight, [up_on, down_on, joined_y, *early])
    last = layered(weight, [(0, 3), (3, 0)])
    mate, third = [down, up, down, up], [down_on, down, up, up_on]
    late = [last, down_on, up_on, last]
    send, held = project_send(layers, grads, weight, third)
    got = lax.ppermute(send, "head", [(0, 1), (1, 0)])
    keep, mate_full, mate_low = project_keep(layers, held, weight, mate, third, [send])
    got_mate = crossed(mate_low, layers, True)
    order = (1, 3, 0, 2)
    last_full, *lows = project_last(order, layers, held, late, [got])
    gots = [crossed(low, layers, False) for low in lows]

    def lanes(array, k):
        return array[:, k * rows : (k + 1) * rows].astype(F32)

    sets = [returned([(keep[r] + lanes(got, r)).astype(BF16) for r in range(INNER)])]
    blocks, after = [None] * INNER, sets[0][1:]
    for k, picks in enumerate((order[:2], order[2:])):
        after = combine(layers, order, picks, last_full, mate_full, got_mate, gots[: k + 1], after)
        for r, block in zip(picks, after):
            blocks[r] = block
    sets.append(returned(blocks))
    tasks = [*((0, r) for r in range(INNER)), (1, 2), (1, 3), (1, 0), (1, 1)]
    blocks = [sets[which][r] for which, r in tasks]
    partly = place(layers, tasks[:-2], blocks[:-2], [], 4 * 10**9)
    return place(layers, tasks[-2:], blocks[-2:], [partly], 1)


def solution(mesh):
    in_specs = (
        P("seq", "head"),
        P("seq", "head"),
        P("seq", "head"),
        P("seq", "head"),
        P("seq", "head"),
        P("head", "seq"),
        P(),
        P("seq", "head"),
        P("seq", "head"),
        P("seq", "head"),
    )
    out_specs = P("seq", "head")
    return jax.shard_map(shards, mesh=mesh, in_specs=in_specs, out_specs=out_specs, check_vma=False)
```

```python
import functools
import math

import jax
import jax.numpy as jnp
from jax import lax
from jax.experimental import pallas as pl
from jax.experimental.pallas import tpu as pltpu
from jax.sharding import PartitionSpec as P

HEAD_SIZE = 128
WINDOW = 512
INNER = 4
LOG2E = 1.4426950408889634
VMEM_LIMIT = 63 * 2**20
JOIN_COST = 10**9 + 1
ATTENTION_COST = 9 * 10**8
F32 = jnp.float32
BF16 = jnp.bfloat16


def attention_kernel(
    group, groups, first_ref, docs_ref, q_ref, do_ref, o_ref, lse_ref,
    k_own_ref, v_own_ref, k_near_ref, v_near_ref, k_far_ref, v_far_ref,
    *refs,
):
    *earlier, dq_ref, own_ref, near_ref, far_ref, probs, dscores, do_rows, q_rows = refs
    tokens = k_own_ref.shape[0]
    per_group = q_ref.shape[1] // HEAD_SIZE
    scale = 1.0 / math.sqrt(HEAD_SIZE)
    rows = lax.broadcasted_iota(jnp.int32, (tokens, tokens), 0)
    cols = lax.broadcasted_iota(jnp.int32, (tokens, tokens), 1)
    causal = rows <= cols
    none = jnp.zeros((tokens, tokens), BF16)
    first = first_ref[0]
    spot = first + lax.broadcasted_iota(jnp.int32, (8, tokens), 1)
    start = jnp.int32(0)
    doc_begin = jnp.zeros((8, tokens), jnp.int32)
    for d in range(docs_ref.shape[0]):
        doc_begin = jnp.maximum(doc_begin, jnp.where(start <= spot, start, 0))
        start = start + docs_ref[d]
    doc_row = doc_begin[0:1]
    mixed = first + rows - jnp.where(causal, 0, 2 * tokens)
    bias_mix = jnp.where(mixed >= doc_row, 0.0, -1e30)
    bias_near = jnp.where(first - tokens + rows >= doc_row, 0.0, -1e30)

    nt = (((1,), (1,)), ((), ()))
    tn = (((0,), (0,)), ((), ()))

    def dot(a, b, dims=(((1,), (0,)), ((), ()))):
        return lax.dot_general(a, b, dims, preferred_element_type=F32)

    keys = jnp.concatenate([k_own_ref[...], k_near_ref[...], k_far_ref[...]], 0)
    values = jnp.concatenate([v_own_ref[...], v_near_ref[...], v_far_ref[...]], 0)
    keys_t = keys.T
    own, near, far = slice(0, tokens), slice(tokens, 2 * tokens), slice(2 * tokens, 3 * tokens)
    def finish(j):
        span = slice(j * HEAD_SIZE, (j + 1) * HEAD_SIZE)
        turn = slice(j * tokens, (j + 1) * tokens)
        dq_ref[:, span] = dot(keys_t, dscores[:, turn]).T.astype(BF16)
        if j % 2:
            two = slice((j - 1) * tokens, (j + 1) * tokens)
        elif j == per_group - 1:
            two = turn
        else:
            return
        sums.append((dot(probs[:, two], do_rows[two, :]), dot(dscores[:, two], q_rows[two, :])))

    sums = []
    for j in range(per_group):
        span = slice(j * HEAD_SIZE, (j + 1) * HEAD_SIZE)
        turn = slice(j * tokens, (j + 1) * tokens)
        q, do, o = q_ref[:, span], do_ref[:, span], o_ref[:, span]
        q_rows[turn, :] = q
        do_rows[turn, :] = do
        head = group * per_group + j
        lse2 = lse_ref[head : head + 1, :] * LOG2E
        delta = jnp.sum((do.astype(F32) * o.astype(F32)).T, axis=0, keepdims=True)
        scores, grads = dot(keys, q, nt), dot(values, do, nt)

        if j:
            finish(j - 1)

        def both(score, grad, bias):
            prob = jnp.exp2(score * (scale * LOG2E) - lse2 + bias)
            return prob.astype(BF16), (prob * (grad - delta) * scale).astype(BF16)

        p_mix, ds_mix = both(
            jnp.where(causal, scores[own], scores[far]),
            jnp.where(causal, grads[own], grads[far]),
            bias_mix,
        )
        p_near, ds_near = both(scores[near], grads[near], bias_near)
        p_own, p_far = jnp.where(causal, p_mix, none), jnp.where(causal, none, p_mix)
        ds_own, ds_far = jnp.where(causal, ds_mix, none), jnp.where(causal, none, ds_mix)
        probs[own, turn], probs[near, turn], probs[far, turn] = p_own, p_near, p_far
        dscores[own, turn], dscores[near, turn], dscores[far, turn] = ds_own, ds_near, ds_far
    finish(per_group - 1)
    acc_v = functools.reduce(lambda a, b: a + b, [each[0] for each in sums])
    acc_k = functools.reduce(lambda a, b: a + b, [each[1] for each in sums])
    for i, ref in enumerate((own_ref, near_ref, far_ref)):
        part = slice(i * tokens, (i + 1) * tokens)
        if group < groups - 1:
            ref[:, :HEAD_SIZE] = acc_k[part].astype(ref.dtype)
            ref[:, HEAD_SIZE:] = acc_v[part].astype(ref.dtype)
            continue
        for g in range(groups):
            k_cols = slice(g * HEAD_SIZE, (g + 1) * HEAD_SIZE)
            v_cols = slice((groups + g) * HEAD_SIZE, (groups + g + 1) * HEAD_SIZE)
            if g == group:
                ref[:, k_cols] = acc_k[part].astype(ref.dtype)
                ref[:, v_cols] = acc_v[part].astype(ref.dtype)
            else:
                ref[:, k_cols] = earlier[3 * g + i][:, :HEAD_SIZE]
                ref[:, v_cols] = earlier[3 * g + i][:, HEAD_SIZE:]


def attention(group, cost, first, doc_lengths, query, output_gradient, output, lse, own, near, far, earlier):
    tokens, width = query.shape
    groups = own.shape[1] // (2 * HEAD_SIZE)
    kv_width = own.shape[1] if group == groups - 1 else 2 * HEAD_SIZE
    part = width // groups
    wide = pl.BlockSpec((tokens, part), lambda i: (0, group))
    per_group = part // HEAD_SIZE
    smem = pl.BlockSpec(memory_space=pltpu.SMEM)
    k_spec = pl.BlockSpec((tokens, HEAD_SIZE), lambda i: (0, group))
    v_spec = pl.BlockSpec((tokens, HEAD_SIZE), lambda i: (0, groups + group))

    def whole(shape):
        return pl.BlockSpec(shape, lambda i: (0, 0))

    return pl.pallas_call(
        functools.partial(attention_kernel, group, groups),
        grid=(1,),
        in_specs=[smem, smem, wide, wide, wide, whole(lse.shape)]
        + [k_spec, v_spec] * 3
        + [whole(array.shape) for array in earlier],
        out_specs=[whole((tokens, part))] + [whole((tokens, kv_width))] * 3,
        out_shape=[
            jax.ShapeDtypeStruct((tokens, part), BF16),
            jax.ShapeDtypeStruct((tokens, kv_width), F32),
            jax.ShapeDtypeStruct((tokens, kv_width), BF16),
            jax.ShapeDtypeStruct((tokens, kv_width), BF16),
        ],
        scratch_shapes=[
            pltpu.VMEM((3 * tokens, per_group * tokens), BF16),
            pltpu.VMEM((3 * tokens, per_group * tokens), BF16),
            pltpu.VMEM((per_group * tokens, HEAD_SIZE), BF16),
            pltpu.VMEM((per_group * tokens, HEAD_SIZE), BF16),
        ],
        compiler_params=pltpu.CompilerParams(vmem_limit_bytes=VMEM_LIMIT),
        cost_estimate=pl.CostEstimate(flops=cost, transcendentals=0, bytes_accessed=1),
        name="attention",
    )(
        first, doc_lengths, query, output_gradient, output, lse,
        own, own, near, near, far, far, *earlier,
    )


NT = (((1,), (1,)), ((), ()))


def grad_copies(grads, held, sems):
    parts = len(grads) // INNER
    tokens = grads[0].shape[0]
    copies = []
    for t in range(INNER):
        lane = 0
        copies.append([])
        for i, grad in enumerate(grads[t * parts : (t + 1) * parts]):
            width = grad.shape[1]
            copies[-1].append(pltpu.make_async_copy(
                grad,
                held.at[t * tokens : (t + 1) * tokens, lane : lane + width],
                sems.at[t * parts + i],
            ))
            lane += width
    for t in range(2):
        for copy in copies[t]:
            copy.start()

    def ready(t):
        for copy in copies[t]:
            copy.wait()
        if t + 2 < INNER:
            for copy in copies[t + 2]:
                copy.start()

    return ready


def standing(layers):
    layer = lax.axis_index("seq") // INNER
    return lax.axis_index("head") == layer // (layers // 2)


def fetch_by_layer(sources, weight, sem):
    layer = lax.axis_index("seq") // INNER
    for z, source in enumerate(sources):
        @pl.when(layer == z)
        def _():
            pltpu.make_async_copy(source, weight, sem).start()


def times(grad, weight):
    return lax.dot_general(grad, weight, NT, preferred_element_type=F32)


def send_kernel(layers, count, *refs):
    grads, (own, *third) = refs[:count], refs[count : count + 1 + layers]
    send, gathered, held, weight, sems = refs[-5:]
    tokens, cols = grads[0].shape[0], weight.shape[0]
    same = standing(layers)

    @pl.when(same)
    def _():
        fetch_by_layer(third, weight, sems.at[count])

    @pl.when(jnp.logical_not(same))
    def _():
        pltpu.make_async_copy(own, weight, sems.at[count]).start()

    ready = grad_copies(grads, held, sems)
    pltpu.make_async_copy(own, weight, sems.at[count]).wait()
    stores = []
    for t in range(INNER):
        ready(t)
        rows = slice(t * tokens, (t + 1) * tokens)
        stores.append(pltpu.make_async_copy(
            held.at[rows], gathered.at[rows], sems.at[count + 1 + t]
        ))
        stores[-1].start()
        lanes = slice(t * cols, (t + 1) * cols)
        send[:, lanes] = times(held[rows, :], weight[...]).astype(BF16)
    for store in stores:
        store.wait()


def keep_kernel(layers, held, own, *refs):
    mate, third = refs[:layers], refs[layers : 2 * layers]
    keep, mate_full, mate_low, weights, sems = refs[-5:]
    cols = weights.shape[1]
    tokens = held.shape[0] // INNER
    same = standing(layers)
    fetch_by_layer(mate, weights.at[1], sems.at[1])

    @pl.when(same)
    def _():
        pltpu.make_async_copy(own, weights.at[0], sems.at[0]).start()

    @pl.when(jnp.logical_not(same))
    def _():
        fetch_by_layer(third, weights.at[0], sems.at[0])

    pltpu.make_async_copy(own, weights.at[1], sems.at[1]).wait()
    for t in range(INNER):
        product = times(held[t * tokens : (t + 1) * tokens, :], weights[1])
        mate_full[t] = product
        mate_low[:, t * cols : (t + 1) * cols] = product.astype(BF16)
    pltpu.make_async_copy(own, weights.at[0], sems.at[0]).wait()
    for t in range(INNER):
        keep[t] = times(held[t * tokens : (t + 1) * tokens, :], weights[0])


def last_kernel(order, layers, held, *refs):
    full, first, second, weight, sem = refs[-5:]
    fetch_by_layer(refs[:layers], weight, sem)
    pltpu.make_async_copy(refs[0], weight, sem).wait()
    tokens, cols = held.shape[0] // INNER, weight.shape[0]
    edge = first.shape[1]
    for k, t in enumerate(order):
        product = times(held[t * tokens : (t + 1) * tokens, :], weight[...])
        full[t] = product
        low = product.astype(BF16)
        lo, hi = k * cols, (k + 1) * cols
        if lo < edge:
            first[:, lo : min(hi, edge)] = low[:, : min(hi, edge) - lo]
        if hi > edge:
            second[:, max(lo, edge) - edge : hi - edge] = low[:, max(lo, edge) - lo :]


def project(kernel, layers, operands, in_vmem, outs, scratch, limit, name):
    vmem = pl.BlockSpec(memory_space=pltpu.VMEM)
    hbm = pl.BlockSpec(memory_space=pltpu.HBM)
    return pl.pallas_call(
        functools.partial(kernel, layers),
        in_specs=[vmem] * in_vmem + [hbm] * (len(operands) - in_vmem),
        out_specs=[vmem if in_place else hbm for in_place, _, _ in outs],
        out_shape=[jax.ShapeDtypeStruct(shape, kind) for _, shape, kind in outs],
        scratch_shapes=scratch,
        compiler_params=pltpu.CompilerParams(vmem_limit_bytes=limit),
        cost_estimate=pl.CostEstimate(flops=1, transcendentals=0, bytes_accessed=1),
        name=name,
    )(*operands)


def project_send(layers, grads, own, third):
    tokens = grads[0].shape[0]
    cols, depth = own.shape
    return project(
        lambda layers, *refs: send_kernel(layers, len(grads), *refs),
        layers,
        [*grads, own, *third],
        0,
        [(True, (tokens, INNER * cols), BF16), (False, (INNER * tokens, depth), BF16)],
        [
            pltpu.VMEM((INNER * tokens, depth), BF16),
            pltpu.VMEM((cols, depth), BF16),
            pltpu.SemaphoreType.DMA((len(grads) + 1 + INNER,)),
        ],
        VMEM_LIMIT,
        "project_send",
    )


def project_keep(layers, gathered, own, mate, third, after):
    tokens, depth = gathered.shape[0] // INNER, gathered.shape[1]
    cols = own.shape[0]
    full = (True, (INNER, tokens, cols), F32)
    return project(
        keep_kernel,
        layers,
        [gathered, own, *mate, *third, *after],
        1,
        [full, full, (True, (tokens, INNER * cols), BF16)],
        [pltpu.VMEM((2, cols, depth), BF16), pltpu.SemaphoreType.DMA((2,))],
        59 * 2**20,
        "project_keep",
    )


def project_last(order, layers, gathered, late, after):
    tokens, cols = gathered.shape[0] // INNER, late[0].shape[0]
    edge = -(-INNER // 2 * cols // HEAD_SIZE) * HEAD_SIZE
    return project(
        functools.partial(last_kernel, order),
        layers,
        [gathered, *late, *after],
        1,
        [
            (True, (INNER, tokens, cols), F32),
            (True, (tokens, edge), BF16),
            (True, (tokens, INNER * cols - edge), BF16),
        ],
        [pltpu.VMEM(late[0].shape, BF16), pltpu.SemaphoreType.DMA],
        10 * 2**20,
        "project_last",
    )


def combine_kernel(layers, order, picks, count, last_full, mate_full, got_mate, *refs):
    gots, outs = refs[:count], refs[-len(picks) :]
    same = standing(layers)
    cols = last_full.shape[2]
    for out, r in zip(outs, picks):
        @pl.when(same)
        def _():
            got = got_mate[:, r * cols : (r + 1) * cols].astype(F32)
            out[...] = (mate_full[r] + got).astype(BF16)

        @pl.when(jnp.logical_not(same))
        def _():
            start, begin = order.index(r) * cols, 0
            for got in gots:
                lo, hi = max(start, begin), min(start + cols, begin + got.shape[1])
                if lo < hi:
                    part = got[:, lo - begin : hi - begin].astype(F32)
                    total = last_full[r, :, lo - start : hi - start] + part
                    out[:, lo - start : hi - start] = total.astype(BF16)
                begin += got.shape[1]


def combine(layers, order, picks, last_full, mate_full, got_mate, gots, after):
    _, tokens, cols = last_full.shape
    vmem = pl.BlockSpec(memory_space=pltpu.VMEM)
    return pl.pallas_call(
        functools.partial(combine_kernel, layers, order, picks, len(gots)),
        in_specs=[vmem] * (3 + len(gots)) + [pl.BlockSpec(memory_space=pltpu.HBM)] * len(after),
        out_specs=[vmem] * len(picks),
        out_shape=[jax.ShapeDtypeStruct((tokens, cols), BF16)] * len(picks),
        compiler_params=pltpu.CompilerParams(vmem_limit_bytes=12 * 2**20),
        cost_estimate=pl.CostEstimate(flops=1, transcendentals=0, bytes_accessed=1),
        name="combine",
    )(last_full, mate_full, got_mate, *gots, *after)


def place_kernel(layers, tasks, *refs):
    out = refs[-1]
    width = refs[0].shape[1]
    if len(refs) > len(tasks) + 1:
        out[...] = refs[-2][...]
    seq = lax.axis_index("seq")
    layer, inner = seq // INNER, seq % INNER
    same = standing(layers)
    lower = layer // (layers // 2) == 0
    first_low = jnp.where(same, layer % 2 == 0, lower)
    for i in range(INNER):
        for low in (True, False):
            @pl.when((inner == i) & (first_low == low))
            def _():
                for block, (which, r) in zip(refs, tasks):
                    lane = ((which == 0) != low) * INNER * width + (r ^ i) * width
                    out[:, lane : lane + width] = block[...]


def place(layers, tasks, blocks, earlier, cost):
    tokens, width = blocks[0].shape
    vmem = pl.BlockSpec(memory_space=pltpu.VMEM)
    return pl.pallas_call(
        functools.partial(place_kernel, layers, tasks),
        in_specs=[vmem] * (len(blocks) + len(earlier)),
        out_specs=vmem,
        out_shape=jax.ShapeDtypeStruct((tokens, 2 * INNER * width), BF16),
        cost_estimate=pl.CostEstimate(flops=cost, transcendentals=0, bytes_accessed=1),
        compiler_params=pltpu.CompilerParams(vmem_limit_bytes=16 * 2**20),
        name="place",
    )(*blocks, *earlier)


def pack_kernel(splits, *refs):
    outs, sems = refs[-1 - len(splits) : -1], refs[-1]
    copies = []
    for out, (lo, hi) in zip(outs, splits):
        lane = 0
        for source in refs[lo:hi]:
            width = source.shape[1]
            copies.append(pltpu.make_async_copy(
                source, out.at[:, lane : lane + width], sems.at[len(copies)]
            ))
            copies[-1].start()
            lane += width
    for copy in copies:
        copy.wait()


def pack(*groups):
    sources, splits = [], []
    for group in groups:
        splits.append((len(sources), len(sources) + len(group)))
        sources += group
    return pl.pallas_call(
        functools.partial(pack_kernel, splits),
        in_specs=[pl.BlockSpec(memory_space=pltpu.HBM)] * len(sources),
        out_specs=[pl.BlockSpec(memory_space=pltpu.VMEM)] * len(groups),
        out_shape=[
            jax.ShapeDtypeStruct((g[0].shape[0], sum(each.shape[1] for each in g)), BF16)
            for g in groups
        ],
        scratch_shapes=[pltpu.SemaphoreType.DMA((len(sources),))],
        compiler_params=pltpu.CompilerParams(vmem_limit_bytes=VMEM_LIMIT),
        cost_estimate=pl.CostEstimate(flops=1, transcendentals=0, bytes_accessed=1),
        name="pack",
    )(*sources)


def gate_kernel(*refs):
    pass


def gate(array, deps, flops=1):
    hbm = pl.BlockSpec(memory_space=pltpu.HBM)
    return pl.pallas_call(
        gate_kernel,
        in_specs=[hbm] * (1 + len(deps)),
        out_specs=hbm,
        out_shape=jax.ShapeDtypeStruct(array.shape, array.dtype),
        input_output_aliases={0: 0},
        compiler_params=pltpu.CompilerParams(vmem_limit_bytes=VMEM_LIMIT),
        cost_estimate=pl.CostEstimate(flops=flops, transcendentals=0, bytes_accessed=1),
        name="gate",
    )(array, *deps)


def is_odd():
    return lax.axis_index("seq") % 2 == 1


def choose_kernel(odd_ref, even_ref, out):
    @pl.when(is_odd())
    def _():
        out[...] = odd_ref[...]

    @pl.when(jnp.logical_not(is_odd()))
    def _():
        out[...] = even_ref[...]


def merge_kernel(far, got, *refs):
    out = refs[-1]
    out[...] = far[...]

    @pl.when(is_odd())
    def _():
        out[...] = (far[...].astype(F32) + got[...].astype(F32)).astype(BF16)


def join_kernel(dq, own, got, back, *refs):
    out = refs[-1]
    width = dq.shape[1]
    out[:, :width] = dq[...]
    total = own[...] + back[...].astype(F32)

    @pl.when(is_odd())
    def _():
        out[:, width:] = total.astype(BF16)

    @pl.when(jnp.logical_not(is_odd()))
    def _():
        out[:, width:] = (total + got[...].astype(F32)).astype(BF16)


def small(kernel, arrays, deps, width, name, limit=6 * 2**20, cost=1):
    vmem = pl.BlockSpec(memory_space=pltpu.VMEM)
    hbm = pl.BlockSpec(memory_space=pltpu.HBM)
    return pl.pallas_call(
        kernel,
        in_specs=[vmem] * len(arrays) + [hbm] * len(deps),
        out_specs=vmem,
        out_shape=jax.ShapeDtypeStruct((arrays[0].shape[0], width), BF16),
        compiler_params=pltpu.CompilerParams(vmem_limit_bytes=limit),
        cost_estimate=pl.CostEstimate(flops=cost, transcendentals=0, bytes_accessed=1),
        name=name,
    )(*arrays, *deps)


def shifted(array, by):
    peers = lax.axis_size("seq")
    pairs = [(i, i + by) for i in range(peers) if 0 <= i + by < peers]
    return lax.ppermute(array, "seq", pairs)


def swapped(array, bits):
    peers = lax.axis_size("seq")
    return lax.ppermute(array, "seq", [(i, i ^ bits) for i in range(peers)])


def layered(array, moves):
    pairs = [(a * INNER + i, b * INNER + i) for a, b in moves for i in range(INNER)]
    return lax.ppermute(array, "seq", pairs)


def crossed(array, layers, inward):
    pairs = []
    for i in range(layers * INNER):
        half = i // INNER // (layers // 2)
        pairs.append((2 * i + 1 - half, 2 * i + half) if inward else (2 * i + half, 2 * i + 1 - half))
    return lax.ppermute(array, ("seq", "head"), pairs)


def returned(blocks):
    return [blocks[0], swapped(blocks[2], 1), swapped(blocks[1], 2), swapped(blocks[3], 3)]


def ordered(blocks, inner):
    cols = []
    for j in range(INNER):
        pick = blocks[j]
        for i in range(1, INNER):
            pick = jnp.where(inner == i, blocks[j ^ i], pick)
        cols.append(pick)
    return jnp.concatenate(cols, 1)


def project_gathered(grads, weight, layers, tokens, head, inner):
    rows = weight.shape[0]
    groups = [[z * INNER + i for z in range(layers)] for i in range(INNER)]
    every = lax.all_gather(weight, "seq", axis=0, tiled=True, axis_index_groups=groups)
    halves = every.reshape(2, layers // 2 * rows, -1)

    def times(piece):
        return lax.dot_general(
            grads, piece, (((1,), (1,)), ((), ())), preferred_element_type=F32
        )

    send = times(jnp.where(head == 0, halves[1], halves[0])).astype(BF16)
    got = lax.ppermute(send, "head", [(0, 1), (1, 0)])
    keep = times(jnp.where(head == 0, halves[0], halves[1]))
    blocks = returned((keep + got.astype(F32)).astype(BF16).reshape(INNER, tokens, -1))
    blocks = [b.reshape(tokens * (layers // 2), rows) for b in blocks]
    return ordered(blocks, inner).reshape(tokens, -1)


def tied(*arrays):
    return lax.optimization_barrier(arrays)


def shards(
    query, key, value, output, output_gradient, lse, doc_lengths, w_query, key_weight, value_weight
):
    tokens = query.shape[0]
    seq = lax.axis_index("seq")
    head = lax.axis_index("head")
    inner = seq % INNER
    layers = lax.axis_size("seq") // INNER
    line = layers == 4

    rows = w_query.shape[0]
    if line:
        pair, weight = pack((key, value), (w_query, key_weight, value_weight))
    else:
        pair = jnp.concatenate([key, value], 1)
        weight = jnp.concatenate([w_query, key_weight, value_weight], 1)
    pair_width = pair.shape[1]
    far = shifted(pair, 2)
    near = swapped(small(choose_kernel, [far, pair], [], pair.shape[1], "choose"), 1)
    if line:
        up = layered(weight, [(0, 1), (1, 2), (2, 3)])
        down = layered(weight, [(1, 0), (2, 1), (3, 2)])
    first = (seq * tokens).astype(jnp.int32).reshape(1)
    groups = key.shape[1] // HEAD_SIZE
    dq, earlier = [], []
    for g in range(groups):
        dq_part, *parts = attention(
            g, ATTENTION_COST, first, doc_lengths, query, output_gradient, output, lse,
            pair, near, far, earlier,
        )
        dq.append(dq_part)
        earlier += parts
    own_part, near_part, far_part = parts
    dq_y = [swapped(part, 2) for part in dq[:-1]]
    if line:
        down = gate(down, dq_y)
        up_on = layered(up, [(1, 2), (2, 3)])
        down_on = layered(down, [(1, 0), (2, 1)])
    got = swapped(near_part, 1)
    back = shifted(small(merge_kernel, [far_part, got], [], pair.shape[1], "merge"), -2)
    deps = [up, down] if line else []
    width = dq[-1].shape[1] + pair.shape[1]
    joined = small(
        join_kernel, [dq[-1], own_part, got, back], deps, width, "join", VMEM_LIMIT, JOIN_COST
    )
    joined_y = swapped(joined, 2)
    grads = [*dq[:-1], joined, *dq_y, joined_y]
    others = [swapped(g, 1) for g in grads]
    grads = grads + others

    if not line:
        parts = len(grads) // INNER
        four = jnp.concatenate(
            [jnp.concatenate(grads[t * parts : (t + 1) * parts], 1) for t in range(INNER)], 0
        )
        return project_gathered(four, weight, layers, tokens, head, inner)

    early = [o for o, g in zip(others, grads) if g is not joined and g is not joined_y]
    weight = gate(weight, [up_on, down_on, joined_y, *early])
    last = layered(weight, [(0, 3), (3, 0)])
    mate, third = [down, up, down, up], [down_on, down, up, up_on]
    late = [last, down_on, up_on, last]
    send, held = project_send(layers, grads, weight, third)
    got = lax.ppermute(send, "head", [(0, 1), (1, 0)])
    keep, mate_full, mate_low = project_keep(layers, held, weight, mate, third, [send])
    got_mate = crossed(mate_low, layers, True)
    order = (1, 3, 0, 2)
    last_full, *lows = project_last(order, layers, held, late, [got])
    gots = [crossed(low, layers, False) for low in lows]

    def lanes(array, k):
        return array[:, k * rows : (k + 1) * rows].astype(F32)

    sets = [returned([(keep[r] + lanes(got, r)).astype(BF16) for r in range(INNER)])]
    blocks, after = [None] * INNER, sets[0][1:]
    for k, picks in enumerate((order[:2], order[2:])):
        after = combine(layers, order, picks, last_full, mate_full, got_mate, gots[: k + 1], after)
        for r, block in zip(picks, after):
            blocks[r] = block
    sets.append(returned(blocks))
    tasks = [*((0, r) for r in range(INNER)), (1, 2), (1, 3), (1, 0), (1, 1)]
    blocks = [sets[which][r] for which, r in tasks]
    partly = place(layers, tasks[:-2], blocks[:-2], [], 4 * 10**9)
    return place(layers, tasks[-2:], blocks[-2:], [partly], 1)


def solution(mesh):
    in_specs = (
        P("seq", "head"),
        P("seq", "head"),
        P("seq", "head"),
        P("seq", "head"),
        P("seq", "head"),
        P("head", "seq"),
        P(),
        P("seq", "head"),
        P("seq", "head"),
        P("seq", "head"),
    )
    out_specs = P("seq", "head")
    return jax.shard_map(shards, mesh=mesh, in_specs=in_specs, out_specs=out_specs, check_vma=False)
```

```python
import functools
import math

import jax
import jax.numpy as jnp
from jax import lax
from jax.experimental import pallas as pl
from jax.experimental.pallas import tpu as pltpu
from jax.sharding import PartitionSpec as P

HEAD_SIZE = 128
WINDOW = 512
INNER = 4
LOG2E = 1.4426950408889634
VMEM_LIMIT = 63 * 2**20
JOIN_COST = 10**9 + 1
ATTENTION_COST = 9 * 10**8
F32 = jnp.float32
BF16 = jnp.bfloat16


def attention_kernel(
    group, groups, first_ref, docs_ref, q_ref, do_ref, o_ref, lse_ref,
    k_own_ref, v_own_ref, k_near_ref, v_near_ref, k_far_ref, v_far_ref,
    *refs,
):
    *earlier, dq_ref, own_ref, near_ref, far_ref, probs, dscores, do_rows, q_rows = refs
    tokens = k_own_ref.shape[0]
    per_group = q_ref.shape[1] // HEAD_SIZE
    scale = 1.0 / math.sqrt(HEAD_SIZE)
    rows = lax.broadcasted_iota(jnp.int32, (tokens, tokens), 0)
    cols = lax.broadcasted_iota(jnp.int32, (tokens, tokens), 1)
    causal = rows <= cols
    none = jnp.zeros((tokens, tokens), BF16)
    first = first_ref[0]
    spot = first + lax.broadcasted_iota(jnp.int32, (8, tokens), 1)
    start = jnp.int32(0)
    doc_begin = jnp.zeros((8, tokens), jnp.int32)
    for d in range(docs_ref.shape[0]):
        doc_begin = jnp.maximum(doc_begin, jnp.where(start <= spot, start, 0))
        start = start + docs_ref[d]
    doc_row = doc_begin[0:1]
    mixed = first + rows - jnp.where(causal, 0, 2 * tokens)
    bias_mix = jnp.where(mixed >= doc_row, 0.0, -1e30)
    bias_near = jnp.where(first - tokens + rows >= doc_row, 0.0, -1e30)

    nt = (((1,), (1,)), ((), ()))
    tn = (((0,), (0,)), ((), ()))

    def dot(a, b, dims=(((1,), (0,)), ((), ()))):
        return lax.dot_general(a, b, dims, preferred_element_type=F32)

    keys = jnp.concatenate([k_own_ref[...], k_near_ref[...], k_far_ref[...]], 0)
    values = jnp.concatenate([v_own_ref[...], v_near_ref[...], v_far_ref[...]], 0)
    keys_t = keys.T
    own, near, far = slice(0, tokens), slice(tokens, 2 * tokens), slice(2 * tokens, 3 * tokens)
    def finish(j):
        span = slice(j * HEAD_SIZE, (j + 1) * HEAD_SIZE)
        turn = slice(j * tokens, (j + 1) * tokens)
        dq_ref[:, span] = dot(keys_t, dscores[:, turn]).T.astype(BF16)
        if j % 2:
            two = slice((j - 1) * tokens, (j + 1) * tokens)
        elif j == per_group - 1:
            two = turn
        else:
            return
        sums.append((dot(probs[:, two], do_rows[two, :]), dot(dscores[:, two], q_rows[two, :])))

    sums = []
    for j in range(per_group):
        span = slice(j * HEAD_SIZE, (j + 1) * HEAD_SIZE)
        turn = slice(j * tokens, (j + 1) * tokens)
        q, do, o = q_ref[:, span], do_ref[:, span], o_ref[:, span]
        q_rows[turn, :] = q
        do_rows[turn, :] = do
        head = group * per_group + j
        lse2 = lse_ref[head : head + 1, :] * LOG2E
        delta = jnp.sum((do.astype(F32) * o.astype(F32)).T, axis=0, keepdims=True)
        scores, grads = dot(keys, q, nt), dot(values, do, nt)

        if j:
            finish(j - 1)

        def both(score, grad, bias):
            prob = jnp.exp2(score * (scale * LOG2E) - lse2 + bias)
            return prob.astype(BF16), (prob * (grad - delta) * scale).astype(BF16)

        p_mix, ds_mix = both(
            jnp.where(causal, scores[own], scores[far]),
            jnp.where(causal, grads[own], grads[far]),
            bias_mix,
        )
        p_near, ds_near = both(scores[near], grads[near], bias_near)
        p_own, p_far = jnp.where(causal, p_mix, none), jnp.where(causal, none, p_mix)
        ds_own, ds_far = jnp.where(causal, ds_mix, none), jnp.where(causal, none, ds_mix)
        probs[own, turn], probs[near, turn], probs[far, turn] = p_own, p_near, p_far
        dscores[own, turn], dscores[near, turn], dscores[far, turn] = ds_own, ds_near, ds_far
    finish(per_group - 1)
    acc_v = functools.reduce(lambda a, b: a + b, [each[0] for each in sums])
    acc_k = functools.reduce(lambda a, b: a + b, [each[1] for each in sums])
    for i, ref in enumerate((own_ref, near_ref, far_ref)):
        part = slice(i * tokens, (i + 1) * tokens)
        if group < groups - 1:
            ref[:, :HEAD_SIZE] = acc_k[part].astype(ref.dtype)
            ref[:, HEAD_SIZE:] = acc_v[part].astype(ref.dtype)
            continue
        for g in range(groups):
            k_cols = slice(g * HEAD_SIZE, (g + 1) * HEAD_SIZE)
            v_cols = slice((groups + g) * HEAD_SIZE, (groups + g + 1) * HEAD_SIZE)
            if g == group:
                ref[:, k_cols] = acc_k[part].astype(ref.dtype)
                ref[:, v_cols] = acc_v[part].astype(ref.dtype)
            else:
                ref[:, k_cols] = earlier[3 * g + i][:, :HEAD_SIZE]
                ref[:, v_cols] = earlier[3 * g + i][:, HEAD_SIZE:]


def attention(group, cost, first, doc_lengths, query, output_gradient, output, lse, own, near, far, earlier):
    tokens, width = query.shape
    groups = own.shape[1] // (2 * HEAD_SIZE)
    kv_width = own.shape[1] if group == groups - 1 else 2 * HEAD_SIZE
    part = width // groups
    wide = pl.BlockSpec((tokens, part), lambda i: (0, group))
    per_group = part // HEAD_SIZE
    smem = pl.BlockSpec(memory_space=pltpu.SMEM)
    k_spec = pl.BlockSpec((tokens, HEAD_SIZE), lambda i: (0, group))
    v_spec = pl.BlockSpec((tokens, HEAD_SIZE), lambda i: (0, groups + group))

    def whole(shape):
        return pl.BlockSpec(shape, lambda i: (0, 0))

    return pl.pallas_call(
        functools.partial(attention_kernel, group, groups),
        grid=(1,),
        in_specs=[smem, smem, wide, wide, wide, whole(lse.shape)]
        + [k_spec, v_spec] * 3
        + [whole(array.shape) for array in earlier],
        out_specs=[whole((tokens, part))] + [whole((tokens, kv_width))] * 3,
        out_shape=[
            jax.ShapeDtypeStruct((tokens, part), BF16),
            jax.ShapeDtypeStruct((tokens, kv_width), F32),
            jax.ShapeDtypeStruct((tokens, kv_width), BF16),
            jax.ShapeDtypeStruct((tokens, kv_width), BF16),
        ],
        scratch_shapes=[
            pltpu.VMEM((3 * tokens, per_group * tokens), BF16),
            pltpu.VMEM((3 * tokens, per_group * tokens), BF16),
            pltpu.VMEM((per_group * tokens, HEAD_SIZE), BF16),
            pltpu.VMEM((per_group * tokens, HEAD_SIZE), BF16),
        ],
        compiler_params=pltpu.CompilerParams(vmem_limit_bytes=VMEM_LIMIT),
        cost_estimate=pl.CostEstimate(flops=cost, transcendentals=0, bytes_accessed=1),
        name="attention",
    )(
        first, doc_lengths, query, output_gradient, output, lse,
        own, own, near, near, far, far, *earlier,
    )


NT = (((1,), (1,)), ((), ()))


def grad_copies(grads, held, sems):
    parts = len(grads) // INNER
    tokens = grads[0].shape[0]
    copies = []
    for t in range(INNER):
        lane = 0
        copies.append([])
        for i, grad in enumerate(grads[t * parts : (t + 1) * parts]):
            width = grad.shape[1]
            copies[-1].append(pltpu.make_async_copy(
                grad,
                held.at[t * tokens : (t + 1) * tokens, lane : lane + width],
                sems.at[t * parts + i],
            ))
            lane += width
    for t in range(2):
        for copy in copies[t]:
            copy.start()

    def ready(t):
        for copy in copies[t]:
            copy.wait()
        if t + 2 < INNER:
            for copy in copies[t + 2]:
                copy.start()

    return ready


def standing(layers):
    layer = lax.axis_index("seq") // INNER
    return lax.axis_index("head") == layer // (layers // 2)


def fetch_by_layer(sources, weight, sem):
    layer = lax.axis_index("seq") // INNER
    for z, source in enumerate(sources):
        @pl.when(layer == z)
        def _():
            pltpu.make_async_copy(source, weight, sem).start()


def times(grad, weight):
    return lax.dot_general(grad, weight, NT, preferred_element_type=F32)


def send_kernel(layers, count, *refs):
    grads, (own, *third) = refs[:count], refs[count : count + 1 + layers]
    send, gathered, held, weight, sems = refs[-5:]
    tokens, cols = grads[0].shape[0], weight.shape[0]
    same = standing(layers)

    @pl.when(same)
    def _():
        fetch_by_layer(third, weight, sems.at[count])

    @pl.when(jnp.logical_not(same))
    def _():
        pltpu.make_async_copy(own, weight, sems.at[count]).start()

    ready = grad_copies(grads, held, sems)
    pltpu.make_async_copy(own, weight, sems.at[count]).wait()
    stores = []
    for t in range(INNER):
        ready(t)
        rows = slice(t * tokens, (t + 1) * tokens)
        stores.append(pltpu.make_async_copy(
            held.at[rows], gathered.at[rows], sems.at[count + 1 + t]
        ))
        stores[-1].start()
        lanes = slice(t * cols, (t + 1) * cols)
        send[:, lanes] = times(held[rows, :], weight[...]).astype(BF16)
    for store in stores:
        store.wait()


def keep_kernel(layers, held, own, *refs):
    mate, third = refs[:layers], refs[layers : 2 * layers]
    keep, mate_full, mate_low, weights, sems = refs[-5:]
    cols = weights.shape[1]
    tokens = held.shape[0] // INNER
    same = standing(layers)
    fetch_by_layer(mate, weights.at[1], sems.at[1])

    @pl.when(same)
    def _():
        pltpu.make_async_copy(own, weights.at[0], sems.at[0]).start()

    @pl.when(jnp.logical_not(same))
    def _():
        fetch_by_layer(third, weights.at[0], sems.at[0])

    pltpu.make_async_copy(own, weights.at[1], sems.at[1]).wait()
    for t in range(INNER):
        product = times(held[t * tokens : (t + 1) * tokens, :], weights[1])
        mate_full[t] = product
        mate_low[:, t * cols : (t + 1) * cols] = product.astype(BF16)
    pltpu.make_async_copy(own, weights.at[0], sems.at[0]).wait()
    for t in range(INNER):
        keep[t] = times(held[t * tokens : (t + 1) * tokens, :], weights[0])


def last_kernel(order, layers, held, *refs):
    full, first, second, weight, sem = refs[-5:]
    fetch_by_layer(refs[:layers], weight, sem)
    pltpu.make_async_copy(refs[0], weight, sem).wait()
    tokens, cols = held.shape[0] // INNER, weight.shape[0]
    edge = first.shape[1]
    for k, t in enumerate(order):
        product = times(held[t * tokens : (t + 1) * tokens, :], weight[...])
        full[t] = product
        low = product.astype(BF16)
        lo, hi = k * cols, (k + 1) * cols
        if lo < edge:
            first[:, lo : min(hi, edge)] = low[:, : min(hi, edge) - lo]
        if hi > edge:
            second[:, max(lo, edge) - edge : hi - edge] = low[:, max(lo, edge) - lo :]


def project(kernel, layers, operands, in_vmem, outs, scratch, limit, name):
    vmem = pl.BlockSpec(memory_space=pltpu.VMEM)
    hbm = pl.BlockSpec(memory_space=pltpu.HBM)
    return pl.pallas_call(
        functools.partial(kernel, layers),
        in_specs=[vmem] * in_vmem + [hbm] * (len(operands) - in_vmem),
        out_specs=[vmem if in_place else hbm for in_place, _, _ in outs],
        out_shape=[jax.ShapeDtypeStruct(shape, kind) for _, shape, kind in outs],
        scratch_shapes=scratch,
        compiler_params=pltpu.CompilerParams(vmem_limit_bytes=limit),
        cost_estimate=pl.CostEstimate(flops=1, transcendentals=0, bytes_accessed=1),
        name=name,
    )(*operands)


def project_send(layers, grads, own, third):
    tokens = grads[0].shape[0]
    cols, depth = own.shape
    return project(
        lambda layers, *refs: send_kernel(layers, len(grads), *refs),
        layers,
        [*grads, own, *third],
        0,
        [(True, (tokens, INNER * cols), BF16), (False, (INNER * tokens, depth), BF16)],
        [
            pltpu.VMEM((INNER * tokens, depth), BF16),
            pltpu.VMEM((cols, depth), BF16),
            pltpu.SemaphoreType.DMA((len(grads) + 1 + INNER,)),
        ],
        VMEM_LIMIT,
        "project_send",
    )


def project_keep(layers, gathered, own, mate, third, after):
    tokens, depth = gathered.shape[0] // INNER, gathered.shape[1]
    cols = own.shape[0]
    full = (True, (INNER, tokens, cols), F32)
    return project(
        keep_kernel,
        layers,
        [gathered, own, *mate, *third, *after],
        1,
        [full, full, (True, (tokens, INNER * cols), BF16)],
        [pltpu.VMEM((2, cols, depth), BF16), pltpu.SemaphoreType.DMA((2,))],
        59 * 2**20,
        "project_keep",
    )


def project_last(order, layers, gathered, late, after):
    tokens, cols = gathered.shape[0] // INNER, late[0].shape[0]
    edge = -(-INNER // 2 * cols // HEAD_SIZE) * HEAD_SIZE
    return project(
        functools.partial(last_kernel, order),
        layers,
        [gathered, *late, *after],
        1,
        [
            (True, (INNER, tokens, cols), F32),
            (True, (tokens, edge), BF16),
            (True, (tokens, INNER * cols - edge), BF16),
        ],
        [pltpu.VMEM(late[0].shape, BF16), pltpu.SemaphoreType.DMA],
        10 * 2**20,
        "project_last",
    )


def combine_kernel(layers, order, picks, count, last_full, mate_full, got_mate, *refs):
    gots, outs = refs[:count], refs[-len(picks) :]
    same = standing(layers)
    cols = last_full.shape[2]
    for out, r in zip(outs, picks):
        @pl.when(same)
        def _():
            got = got_mate[:, r * cols : (r + 1) * cols].astype(F32)
            out[...] = (mate_full[r] + got).astype(BF16)

        @pl.when(jnp.logical_not(same))
        def _():
            start, begin = order.index(r) * cols, 0
            for got in gots:
                lo, hi = max(start, begin), min(start + cols, begin + got.shape[1])
                if lo < hi:
                    part = got[:, lo - begin : hi - begin].astype(F32)
                    total = last_full[r, :, lo - start : hi - start] + part
                    out[:, lo - start : hi - start] = total.astype(BF16)
                begin += got.shape[1]


def combine(layers, order, picks, last_full, mate_full, got_mate, gots, after):
    _, tokens, cols = last_full.shape
    vmem = pl.BlockSpec(memory_space=pltpu.VMEM)
    return pl.pallas_call(
        functools.partial(combine_kernel, layers, order, picks, len(gots)),
        in_specs=[vmem] * (3 + len(gots)) + [pl.BlockSpec(memory_space=pltpu.HBM)] * len(after),
        out_specs=[vmem] * len(picks),
        out_shape=[jax.ShapeDtypeStruct((tokens, cols), BF16)] * len(picks),
        compiler_params=pltpu.CompilerParams(vmem_limit_bytes=12 * 2**20),
        cost_estimate=pl.CostEstimate(flops=1, transcendentals=0, bytes_accessed=1),
        name="combine",
    )(last_full, mate_full, got_mate, *gots, *after)


def place_kernel(layers, tasks, *refs):
    out = refs[-1]
    width = refs[0].shape[1]
    if len(refs) > len(tasks) + 1:
        out[...] = refs[-2][...]
    seq = lax.axis_index("seq")
    layer, inner = seq // INNER, seq % INNER
    same = standing(layers)
    lower = layer // (layers // 2) == 0
    first_low = jnp.where(same, layer % 2 == 0, lower)
    for i in range(INNER):
        for low in (True, False):
            @pl.when((inner == i) & (first_low == low))
            def _():
                for block, (which, r) in zip(refs, tasks):
                    lane = ((which == 0) != low) * INNER * width + (r ^ i) * width
                    out[:, lane : lane + width] = block[...]


def place(layers, tasks, blocks, earlier, cost):
    tokens, width = blocks[0].shape
    vmem = pl.BlockSpec(memory_space=pltpu.VMEM)
    return pl.pallas_call(
        functools.partial(place_kernel, layers, tasks),
        in_specs=[vmem] * (len(blocks) + len(earlier)),
        out_specs=vmem,
        out_shape=jax.ShapeDtypeStruct((tokens, 2 * INNER * width), BF16),
        cost_estimate=pl.CostEstimate(flops=cost, transcendentals=0, bytes_accessed=1),
        compiler_params=pltpu.CompilerParams(vmem_limit_bytes=16 * 2**20),
        name="place",
    )(*blocks, *earlier)


def pack_kernel(splits, *refs):
    outs, sems = refs[-1 - len(splits) : -1], refs[-1]
    copies = []
    for out, (lo, hi) in zip(outs, splits):
        lane = 0
        for source in refs[lo:hi]:
            width = source.shape[1]
            copies.append(pltpu.make_async_copy(
                source, out.at[:, lane : lane + width], sems.at[len(copies)]
            ))
            copies[-1].start()
            lane += width
    for copy in copies:
        copy.wait()


def pack(*groups):
    sources, splits = [], []
    for group in groups:
        splits.append((len(sources), len(sources) + len(group)))
        sources += group
    return pl.pallas_call(
        functools.partial(pack_kernel, splits),
        in_specs=[pl.BlockSpec(memory_space=pltpu.HBM)] * len(sources),
        out_specs=[pl.BlockSpec(memory_space=pltpu.VMEM)] * len(groups),
        out_shape=[
            jax.ShapeDtypeStruct((g[0].shape[0], sum(each.shape[1] for each in g)), BF16)
            for g in groups
        ],
        scratch_shapes=[pltpu.SemaphoreType.DMA((len(sources),))],
        compiler_params=pltpu.CompilerParams(vmem_limit_bytes=VMEM_LIMIT),
        cost_estimate=pl.CostEstimate(flops=1, transcendentals=0, bytes_accessed=1),
        name="pack",
    )(*sources)


def gate_kernel(*refs):
    pass


def gate(array, deps, flops=1):
    hbm = pl.BlockSpec(memory_space=pltpu.HBM)
    return pl.pallas_call(
        gate_kernel,
        in_specs=[hbm] * (1 + len(deps)),
        out_specs=hbm,
        out_shape=jax.ShapeDtypeStruct(array.shape, array.dtype),
        input_output_aliases={0: 0},
        compiler_params=pltpu.CompilerParams(vmem_limit_bytes=VMEM_LIMIT),
        cost_estimate=pl.CostEstimate(flops=flops, transcendentals=0, bytes_accessed=1),
        name="gate",
    )(array, *deps)


def is_odd():
    return lax.axis_index("seq") % 2 == 1


def choose_kernel(odd_ref, even_ref, out):
    @pl.when(is_odd())
    def _():
        out[...] = odd_ref[...]

    @pl.when(jnp.logical_not(is_odd()))
    def _():
        out[...] = even_ref[...]


def merge_kernel(far, got, *refs):
    out = refs[-1]
    out[...] = far[...]

    @pl.when(is_odd())
    def _():
        out[...] = (far[...].astype(F32) + got[...].astype(F32)).astype(BF16)


def join_kernel(dq, own, got, back, *refs):
    out = refs[-1]
    width = dq.shape[1]
    out[:, :width] = dq[...]
    total = own[...] + back[...].astype(F32)

    @pl.when(is_odd())
    def _():
        out[:, width:] = total.astype(BF16)

    @pl.when(jnp.logical_not(is_odd()))
    def _():
        out[:, width:] = (total + got[...].astype(F32)).astype(BF16)


def small(kernel, arrays, deps, width, name, limit=6 * 2**20, cost=1):
    vmem = pl.BlockSpec(memory_space=pltpu.VMEM)
    hbm = pl.BlockSpec(memory_space=pltpu.HBM)
    return pl.pallas_call(
        kernel,
        in_specs=[vmem] * len(arrays) + [hbm] * len(deps),
        out_specs=vmem,
        out_shape=jax.ShapeDtypeStruct((arrays[0].shape[0], width), BF16),
        compiler_params=pltpu.CompilerParams(vmem_limit_bytes=limit),
        cost_estimate=pl.CostEstimate(flops=cost, transcendentals=0, bytes_accessed=1),
        name=name,
    )(*arrays, *deps)


def shifted(array, by):
    peers = lax.axis_size("seq")
    pairs = [(i, i + by) for i in range(peers) if 0 <= i + by < peers]
    return lax.ppermute(array, "seq", pairs)


def swapped(array, bits):
    peers = lax.axis_size("seq")
    return lax.ppermute(array, "seq", [(i, i ^ bits) for i in range(peers)])


def layered(array, moves):
    pairs = [(a * INNER + i, b * INNER + i) for a, b in moves for i in range(INNER)]
    return lax.ppermute(array, "seq", pairs)


def crossed(array, layers, inward):
    pairs = []
    for i in range(layers * INNER):
        half = i // INNER // (layers // 2)
        pairs.append((2 * i + 1 - half, 2 * i + half) if inward else (2 * i + half, 2 * i + 1 - half))
    return lax.ppermute(array, ("seq", "head"), pairs)


def returned(blocks):
    return [blocks[0], swapped(blocks[2], 1), swapped(blocks[1], 2), swapped(blocks[3], 3)]


def ordered(blocks, inner):
    cols = []
    for j in range(INNER):
        pick = blocks[j]
        for i in range(1, INNER):
            pick = jnp.where(inner == i, blocks[j ^ i], pick)
        cols.append(pick)
    return jnp.concatenate(cols, 1)


def project_gathered(grads, weight, layers, tokens, head, inner):
    rows = weight.shape[0]
    groups = [[z * INNER + i for z in range(layers)] for i in range(INNER)]
    every = lax.all_gather(weight, "seq", axis=0, tiled=True, axis_index_groups=groups)
    halves = every.reshape(2, layers // 2 * rows, -1)

    def times(piece):
        return lax.dot_general(
            grads, piece, (((1,), (1,)), ((), ())), preferred_element_type=F32
        )

    send = times(jnp.where(head == 0, halves[1], halves[0])).astype(BF16)
    got = lax.ppermute(send, "head", [(0, 1), (1, 0)])
    keep = times(jnp.where(head == 0, halves[0], halves[1]))
    blocks = returned((keep + got.astype(F32)).astype(BF16).reshape(INNER, tokens, -1))
    blocks = [b.reshape(tokens * (layers // 2), rows) for b in blocks]
    return ordered(blocks, inner).reshape(tokens, -1)


def tied(*arrays):
    return lax.optimization_barrier(arrays)


def shards(
    query, key, value, output, output_gradient, lse, doc_lengths, w_query, key_weight, value_weight
):
    tokens = query.shape[0]
    seq = lax.axis_index("seq")
    head = lax.axis_index("head")
    inner = seq % INNER
    layers = lax.axis_size("seq") // INNER
    line = layers == 4

    rows = w_query.shape[0]
    if line:
        pair, weight = pack((key, value), (w_query, key_weight, value_weight))
    else:
        pair = jnp.concatenate([key, value], 1)
        weight = jnp.concatenate([w_query, key_weight, value_weight], 1)
    pair_width = pair.shape[1]
    far = shifted(pair, 2)
    near = swapped(small(choose_kernel, [far, pair], [], pair.shape[1], "choose"), 1)
    if line:
        up = layered(weight, [(0, 1), (1, 2), (2, 3)])
        down = layered(weight, [(1, 0), (2, 1), (3, 2)])
    first = (seq * tokens).astype(jnp.int32).reshape(1)
    groups = key.shape[1] // HEAD_SIZE
    dq, earlier = [], []
    for g in range(groups):
        dq_part, *parts = attention(
            g, ATTENTION_COST, first, doc_lengths, query, output_gradient, output, lse,
            pair, near, far, earlier,
        )
        dq.append(dq_part)
        earlier += parts
    own_part, near_part, far_part = parts
    dq_y = [swapped(part, 2) for part in dq[:-1]]
    if line:
        down = gate(down, dq_y)
        up_on = layered(up, [(1, 2), (2, 3)])
        down_on = layered(down, [(1, 0), (2, 1)])
    got = swapped(near_part, 1)
    back = shifted(small(merge_kernel, [far_part, got], [], pair.shape[1], "merge"), -2)
    deps = [up, down] if line else []
    width = dq[-1].shape[1] + pair.shape[1]
    joined = small(
        join_kernel, [dq[-1], own_part, got, back], deps, width, "join", VMEM_LIMIT, JOIN_COST
    )
    joined_y = swapped(joined, 2)
    grads = [*dq[:-1], joined, *dq_y, joined_y]
    others = [swapped(g, 1) for g in grads]
    grads = grads + others

    if not line:
        parts = len(grads) // INNER
        four = jnp.concatenate(
            [jnp.concatenate(grads[t * parts : (t + 1) * parts], 1) for t in range(INNER)], 0
        )
        return project_gathered(four, weight, layers, tokens, head, inner)

    early = [o for o, g in zip(others, grads) if g is not joined and g is not joined_y]
    weight = gate(weight, [up_on, down_on, joined_y, *early])
    last = layered(weight, [(0, 3), (3, 0)])
    mate, third = [down, up, down, up], [down_on, down, up, up_on]
    late = [last, down_on, up_on, last]
    send, held = project_send(layers, grads, weight, third)
    got = lax.ppermute(send, "head", [(0, 1), (1, 0)])
    keep, mate_full, mate_low = project_keep(layers, held, weight, mate, third, [send])
    got_mate = crossed(mate_low, layers, True)
    order = (1, 3, 0, 2)
    last_full, *lows = project_last(order, layers, held, late, [got])
    gots = [crossed(low, layers, False) for low in lows]

    def lanes(array, k):
        return array[:, k * rows : (k + 1) * rows].astype(F32)

    sets = [returned([(keep[r] + lanes(got, r)).astype(BF16) for r in range(INNER)])]
    blocks, after = [None] * INNER, sets[0][1:2]
    for k, picks in enumerate((order[:2], order[2:])):
        after = combine(layers, order, picks, last_full, mate_full, got_mate, gots[: k + 1], after)
        for r, block in zip(picks, after):
            blocks[r] = block
    sets.append(returned(blocks))
    tasks = [*((0, r) for r in range(INNER)), (1, 2), (1, 3), (1, 0), (1, 1)]
    blocks = [sets[which][r] for which, r in tasks]
    partly = place(layers, tasks[:-2], blocks[:-2], [], 4 * 10**9)
    return place(layers, tasks[-2:], blocks[-2:], [partly], 1)


def solution(mesh):
    in_specs = (
        P("seq", "head"),
        P("seq", "head"),
        P("seq", "head"),
        P("seq", "head"),
        P("seq", "head"),
        P("head", "seq"),
        P(),
        P("seq", "head"),
        P("seq", "head"),
        P("seq", "head"),
    )
    out_specs = P("seq", "head")
    return jax.shard_map(shards, mesh=mesh, in_specs=in_specs, out_specs=out_specs, check_vma=False)
```

```python
import functools
import math

import jax
import jax.numpy as jnp
from jax import lax
from jax.experimental import pallas as pl
from jax.experimental.pallas import tpu as pltpu
from jax.sharding import PartitionSpec as P

HEAD_SIZE = 128
WINDOW = 512
INNER = 4
LOG2E = 1.4426950408889634
VMEM_LIMIT = 63 * 2**20
JOIN_COST = 10**9 + 1
ATTENTION_COST = 9 * 10**8
F32 = jnp.float32
BF16 = jnp.bfloat16


def attention_kernel(
    group, groups, first_ref, docs_ref, q_ref, do_ref, o_ref, lse_ref,
    k_own_ref, v_own_ref, k_near_ref, v_near_ref, k_far_ref, v_far_ref,
    *refs,
):
    *earlier, dq_ref, own_ref, near_ref, far_ref, probs, dscores, do_rows, q_rows = refs
    tokens = k_own_ref.shape[0]
    per_group = q_ref.shape[1] // HEAD_SIZE
    scale = 1.0 / math.sqrt(HEAD_SIZE)
    rows = lax.broadcasted_iota(jnp.int32, (tokens, tokens), 0)
    cols = lax.broadcasted_iota(jnp.int32, (tokens, tokens), 1)
    causal = rows <= cols
    none = jnp.zeros((tokens, tokens), BF16)
    first = first_ref[0]
    spot = first + lax.broadcasted_iota(jnp.int32, (8, tokens), 1)
    start = jnp.int32(0)
    doc_begin = jnp.zeros((8, tokens), jnp.int32)
    for d in range(docs_ref.shape[0]):
        doc_begin = jnp.maximum(doc_begin, jnp.where(start <= spot, start, 0))
        start = start + docs_ref[d]
    doc_row = doc_begin[0:1]
    mixed = first + rows - jnp.where(causal, 0, 2 * tokens)
    bias_mix = jnp.where(mixed >= doc_row, 0.0, -1e30)
    bias_near = jnp.where(first - tokens + rows >= doc_row, 0.0, -1e30)

    nt = (((1,), (1,)), ((), ()))
    tn = (((0,), (0,)), ((), ()))

    def dot(a, b, dims=(((1,), (0,)), ((), ()))):
        return lax.dot_general(a, b, dims, preferred_element_type=F32)

    keys = jnp.concatenate([k_own_ref[...], k_near_ref[...], k_far_ref[...]], 0)
    values = jnp.concatenate([v_own_ref[...], v_near_ref[...], v_far_ref[...]], 0)
    keys_t = keys.T
    own, near, far = slice(0, tokens), slice(tokens, 2 * tokens), slice(2 * tokens, 3 * tokens)
    def finish(j):
        span = slice(j * HEAD_SIZE, (j + 1) * HEAD_SIZE)
        turn = slice(j * tokens, (j + 1) * tokens)
        dq_ref[:, span] = dot(keys_t, dscores[:, turn]).T.astype(BF16)
        if j % 2:
            two = slice((j - 1) * tokens, (j + 1) * tokens)
        elif j == per_group - 1:
            two = turn
        else:
            return
        sums.append((dot(probs[:, two], do_rows[two, :]), dot(dscores[:, two], q_rows[two, :])))

    sums = []
    for j in range(per_group):
        span = slice(j * HEAD_SIZE, (j + 1) * HEAD_SIZE)
        turn = slice(j * tokens, (j + 1) * tokens)
        q, do, o = q_ref[:, span], do_ref[:, span], o_ref[:, span]
        q_rows[turn, :] = q
        do_rows[turn, :] = do
        head = group * per_group + j
        lse2 = lse_ref[head : head + 1, :] * LOG2E
        delta = jnp.sum((do.astype(F32) * o.astype(F32)).T, axis=0, keepdims=True)
        scores, grads = dot(keys, q, nt), dot(values, do, nt)

        if j:
            finish(j - 1)

        def both(score, grad, bias):
            prob = jnp.exp2(score * (scale * LOG2E) - lse2 + bias)
            return prob.astype(BF16), (prob * (grad - delta) * scale).astype(BF16)

        p_mix, ds_mix = both(
            jnp.where(causal, scores[own], scores[far]),
            jnp.where(causal, grads[own], grads[far]),
            bias_mix,
        )
        p_near, ds_near = both(scores[near], grads[near], bias_near)
        p_own, p_far = jnp.where(causal, p_mix, none), jnp.where(causal, none, p_mix)
        ds_own, ds_far = jnp.where(causal, ds_mix, none), jnp.where(causal, none, ds_mix)
        probs[own, turn], probs[near, turn], probs[far, turn] = p_own, p_near, p_far
        dscores[own, turn], dscores[near, turn], dscores[far, turn] = ds_own, ds_near, ds_far
    finish(per_group - 1)
    acc_v = functools.reduce(lambda a, b: a + b, [each[0] for each in sums])
    acc_k = functools.reduce(lambda a, b: a + b, [each[1] for each in sums])
    for i, ref in enumerate((own_ref, near_ref, far_ref)):
        part = slice(i * tokens, (i + 1) * tokens)
        if group < groups - 1:
            ref[:, :HEAD_SIZE] = acc_k[part].astype(ref.dtype)
            ref[:, HEAD_SIZE:] = acc_v[part].astype(ref.dtype)
            continue
        for g in range(groups):
            k_cols = slice(g * HEAD_SIZE, (g + 1) * HEAD_SIZE)
            v_cols = slice((groups + g) * HEAD_SIZE, (groups + g + 1) * HEAD_SIZE)
            if g == group:
                ref[:, k_cols] = acc_k[part].astype(ref.dtype)
                ref[:, v_cols] = acc_v[part].astype(ref.dtype)
            else:
                ref[:, k_cols] = earlier[3 * g + i][:, :HEAD_SIZE]
                ref[:, v_cols] = earlier[3 * g + i][:, HEAD_SIZE:]


def attention(group, cost, first, doc_lengths, query, output_gradient, output, lse, own, near, far, earlier):
    tokens, width = query.shape
    groups = own.shape[1] // (2 * HEAD_SIZE)
    kv_width = own.shape[1] if group == groups - 1 else 2 * HEAD_SIZE
    part = width // groups
    wide = pl.BlockSpec((tokens, part), lambda i: (0, group))
    per_group = part // HEAD_SIZE
    smem = pl.BlockSpec(memory_space=pltpu.SMEM)
    k_spec = pl.BlockSpec((tokens, HEAD_SIZE), lambda i: (0, group))
    v_spec = pl.BlockSpec((tokens, HEAD_SIZE), lambda i: (0, groups + group))

    def whole(shape):
        return pl.BlockSpec(shape, lambda i: (0, 0))

    return pl.pallas_call(
        functools.partial(attention_kernel, group, groups),
        grid=(1,),
        in_specs=[smem, smem, wide, wide, wide, whole(lse.shape)]
        + [k_spec, v_spec] * 3
        + [whole(array.shape) for array in earlier],
        out_specs=[whole((tokens, part))] + [whole((tokens, kv_width))] * 3,
        out_shape=[
            jax.ShapeDtypeStruct((tokens, part), BF16),
            jax.ShapeDtypeStruct((tokens, kv_width), F32),
            jax.ShapeDtypeStruct((tokens, kv_width), BF16),
            jax.ShapeDtypeStruct((tokens, kv_width), BF16),
        ],
        scratch_shapes=[
            pltpu.VMEM((3 * tokens, per_group * tokens), BF16),
            pltpu.VMEM((3 * tokens, per_group * tokens), BF16),
            pltpu.VMEM((per_group * tokens, HEAD_SIZE), BF16),
            pltpu.VMEM((per_group * tokens, HEAD_SIZE), BF16),
        ],
        compiler_params=pltpu.CompilerParams(vmem_limit_bytes=VMEM_LIMIT),
        cost_estimate=pl.CostEstimate(flops=cost, transcendentals=0, bytes_accessed=1),
        name="attention",
    )(
        first, doc_lengths, query, output_gradient, output, lse,
        own, own, near, near, far, far, *earlier,
    )


NT = (((1,), (1,)), ((), ()))


def grad_copies(grads, held, sems):
    parts = len(grads) // INNER
    tokens = grads[0].shape[0]
    copies = []
    for t in range(INNER):
        lane = 0
        copies.append([])
        for i, grad in enumerate(grads[t * parts : (t + 1) * parts]):
            width = grad.shape[1]
            copies[-1].append(pltpu.make_async_copy(
                grad,
                held.at[t * tokens : (t + 1) * tokens, lane : lane + width],
                sems.at[t * parts + i],
            ))
            lane += width
    for t in range(2):
        for copy in copies[t]:
            copy.start()

    def ready(t):
        for copy in copies[t]:
            copy.wait()
        if t + 2 < INNER:
            for copy in copies[t + 2]:
                copy.start()

    return ready


def standing(layers):
    layer = lax.axis_index("seq") // INNER
    return lax.axis_index("head") == layer // (layers // 2)


def fetch_by_layer(sources, weight, sem):
    layer = lax.axis_index("seq") // INNER
    for z, source in enumerate(sources):
        @pl.when(layer == z)
        def _():
            pltpu.make_async_copy(source, weight, sem).start()


def times(grad, weight):
    return lax.dot_general(grad, weight, NT, preferred_element_type=F32)


def send_kernel(layers, count, *refs):
    grads, (own, *third) = refs[:count], refs[count : count + 1 + layers]
    send, gathered, held, weight, sems = refs[-5:]
    tokens, cols = grads[0].shape[0], weight.shape[0]
    same = standing(layers)

    @pl.when(same)
    def _():
        fetch_by_layer(third, weight, sems.at[count])

    @pl.when(jnp.logical_not(same))
    def _():
        pltpu.make_async_copy(own, weight, sems.at[count]).start()

    ready = grad_copies(grads, held, sems)
    pltpu.make_async_copy(own, weight, sems.at[count]).wait()
    stores = []
    for t in range(INNER):
        ready(t)
        rows = slice(t * tokens, (t + 1) * tokens)
        stores.append(pltpu.make_async_copy(
            held.at[rows], gathered.at[rows], sems.at[count + 1 + t]
        ))
        stores[-1].start()
        lanes = slice(t * cols, (t + 1) * cols)
        send[:, lanes] = times(held[rows, :], weight[...]).astype(BF16)
    for store in stores:
        store.wait()


def keep_kernel(layers, held, own, *refs):
    mate, third = refs[:layers], refs[layers : 2 * layers]
    keep, mate_full, mate_low, weights, sems = refs[-5:]
    cols = weights.shape[1]
    tokens = held.shape[0] // INNER
    same = standing(layers)
    fetch_by_layer(mate, weights.at[1], sems.at[1])

    @pl.when(same)
    def _():
        pltpu.make_async_copy(own, weights.at[0], sems.at[0]).start()

    @pl.when(jnp.logical_not(same))
    def _():
        fetch_by_layer(third, weights.at[0], sems.at[0])

    pltpu.make_async_copy(own, weights.at[1], sems.at[1]).wait()
    for t in range(INNER):
        product = times(held[t * tokens : (t + 1) * tokens, :], weights[1])
        mate_full[t] = product
        mate_low[:, t * cols : (t + 1) * cols] = product.astype(BF16)
    pltpu.make_async_copy(own, weights.at[0], sems.at[0]).wait()
    for t in range(INNER):
        keep[t] = times(held[t * tokens : (t + 1) * tokens, :], weights[0])


def last_kernel(order, layers, held, *refs):
    full, first, second, weight, sem = refs[-5:]
    fetch_by_layer(refs[:layers], weight, sem)
    pltpu.make_async_copy(refs[0], weight, sem).wait()
    tokens, cols = held.shape[0] // INNER, weight.shape[0]
    edge = first.shape[1]
    for k, t in enumerate(order):
        product = times(held[t * tokens : (t + 1) * tokens, :], weight[...])
        full[t] = product
        low = product.astype(BF16)
        lo, hi = k * cols, (k + 1) * cols
        if lo < edge:
            first[:, lo : min(hi, edge)] = low[:, : min(hi, edge) - lo]
        if hi > edge:
            second[:, max(lo, edge) - edge : hi - edge] = low[:, max(lo, edge) - lo :]


def project(kernel, layers, operands, in_vmem, outs, scratch, limit, name):
    vmem = pl.BlockSpec(memory_space=pltpu.VMEM)
    hbm = pl.BlockSpec(memory_space=pltpu.HBM)
    return pl.pallas_call(
        functools.partial(kernel, layers),
        in_specs=[vmem] * in_vmem + [hbm] * (len(operands) - in_vmem),
        out_specs=[vmem if in_place else hbm for in_place, _, _ in outs],
        out_shape=[jax.ShapeDtypeStruct(shape, kind) for _, shape, kind in outs],
        scratch_shapes=scratch,
        compiler_params=pltpu.CompilerParams(vmem_limit_bytes=limit),
        cost_estimate=pl.CostEstimate(flops=1, transcendentals=0, bytes_accessed=1),
        name=name,
    )(*operands)


def project_send(layers, grads, own, third):
    tokens = grads[0].shape[0]
    cols, depth = own.shape
    return project(
        lambda layers, *refs: send_kernel(layers, len(grads), *refs),
        layers,
        [*grads, own, *third],
        0,
        [(True, (tokens, INNER * cols), BF16), (False, (INNER * tokens, depth), BF16)],
        [
            pltpu.VMEM((INNER * tokens, depth), BF16),
            pltpu.VMEM((cols, depth), BF16),
            pltpu.SemaphoreType.DMA((len(grads) + 1 + INNER,)),
        ],
        VMEM_LIMIT,
        "project_send",
    )


def project_keep(layers, gathered, own, mate, third, after):
    tokens, depth = gathered.shape[0] // INNER, gathered.shape[1]
    cols = own.shape[0]
    full = (True, (INNER, tokens, cols), F32)
    return project(
        keep_kernel,
        layers,
        [gathered, own, *mate, *third, *after],
        1,
        [full, full, (True, (tokens, INNER * cols), BF16)],
        [pltpu.VMEM((2, cols, depth), BF16), pltpu.SemaphoreType.DMA((2,))],
        59 * 2**20,
        "project_keep",
    )


def project_last(order, layers, gathered, late, after):
    tokens, cols = gathered.shape[0] // INNER, late[0].shape[0]
    edge = -(-INNER // 2 * cols // HEAD_SIZE) * HEAD_SIZE
    return project(
        functools.partial(last_kernel, order),
        layers,
        [gathered, *late, *after],
        1,
        [
            (True, (INNER, tokens, cols), F32),
            (True, (tokens, edge), BF16),
            (True, (tokens, INNER * cols - edge), BF16),
        ],
        [pltpu.VMEM(late[0].shape, BF16), pltpu.SemaphoreType.DMA],
        10 * 2**20,
        "project_last",
    )


def combine_kernel(layers, order, picks, count, last_full, mate_full, got_mate, *refs):
    gots, outs = refs[:count], refs[-len(picks) :]
    same = standing(layers)
    cols = last_full.shape[2]
    for out, r in zip(outs, picks):
        @pl.when(same)
        def _():
            got = got_mate[:, r * cols : (r + 1) * cols].astype(F32)
            out[...] = (mate_full[r] + got).astype(BF16)

        @pl.when(jnp.logical_not(same))
        def _():
            start, begin = order.index(r) * cols, 0
            for got in gots:
                lo, hi = max(start, begin), min(start + cols, begin + got.shape[1])
                if lo < hi:
                    part = got[:, lo - begin : hi - begin].astype(F32)
                    total = last_full[r, :, lo - start : hi - start] + part
                    out[:, lo - start : hi - start] = total.astype(BF16)
                begin += got.shape[1]


def combine(layers, order, picks, last_full, mate_full, got_mate, gots, after):
    _, tokens, cols = last_full.shape
    vmem = pl.BlockSpec(memory_space=pltpu.VMEM)
    return pl.pallas_call(
        functools.partial(combine_kernel, layers, order, picks, len(gots)),
        in_specs=[vmem] * (3 + len(gots)) + [pl.BlockSpec(memory_space=pltpu.HBM)] * len(after),
        out_specs=[vmem] * len(picks),
        out_shape=[jax.ShapeDtypeStruct((tokens, cols), BF16)] * len(picks),
        compiler_params=pltpu.CompilerParams(vmem_limit_bytes=12 * 2**20),
        cost_estimate=pl.CostEstimate(flops=1, transcendentals=0, bytes_accessed=1),
        name="combine",
    )(last_full, mate_full, got_mate, *gots, *after)


def place_kernel(layers, tasks, *refs):
    out = refs[-1]
    width = refs[0].shape[1]
    if len(refs) > len(tasks) + 1:
        out[...] = refs[-2][...]
    seq = lax.axis_index("seq")
    layer, inner = seq // INNER, seq % INNER
    same = standing(layers)
    lower = layer // (layers // 2) == 0
    first_low = jnp.where(same, layer % 2 == 0, lower)
    for i in range(INNER):
        for low in (True, False):
            @pl.when((inner == i) & (first_low == low))
            def _():
                for block, (which, r) in zip(refs, tasks):
                    lane = ((which == 0) != low) * INNER * width + (r ^ i) * width
                    out[:, lane : lane + width] = block[...]


def place(layers, tasks, blocks, earlier, cost):
    tokens, width = blocks[0].shape
    vmem = pl.BlockSpec(memory_space=pltpu.VMEM)
    return pl.pallas_call(
        functools.partial(place_kernel, layers, tasks),
        in_specs=[vmem] * (len(blocks) + len(earlier)),
        out_specs=vmem,
        out_shape=jax.ShapeDtypeStruct((tokens, 2 * INNER * width), BF16),
        cost_estimate=pl.CostEstimate(flops=cost, transcendentals=0, bytes_accessed=1),
        compiler_params=pltpu.CompilerParams(vmem_limit_bytes=16 * 2**20),
        name="place",
    )(*blocks, *earlier)


def pack_kernel(splits, *refs):
    outs, sems = refs[-1 - len(splits) : -1], refs[-1]
    copies = []
    for out, (lo, hi) in zip(outs, splits):
        lane = 0
        for source in refs[lo:hi]:
            width = source.shape[1]
            copies.append(pltpu.make_async_copy(
                source, out.at[:, lane : lane + width], sems.at[len(copies)]
            ))
            copies[-1].start()
            lane += width
    for copy in copies:
        copy.wait()


def pack(*groups):
    sources, splits = [], []
    for group in groups:
        splits.append((len(sources), len(sources) + len(group)))
        sources += group
    return pl.pallas_call(
        functools.partial(pack_kernel, splits),
        in_specs=[pl.BlockSpec(memory_space=pltpu.HBM)] * len(sources),
        out_specs=[pl.BlockSpec(memory_space=pltpu.VMEM)] * len(groups),
        out_shape=[
            jax.ShapeDtypeStruct((g[0].shape[0], sum(each.shape[1] for each in g)), BF16)
            for g in groups
        ],
        scratch_shapes=[pltpu.SemaphoreType.DMA((len(sources),))],
        compiler_params=pltpu.CompilerParams(vmem_limit_bytes=VMEM_LIMIT),
        cost_estimate=pl.CostEstimate(flops=1, transcendentals=0, bytes_accessed=1),
        name="pack",
    )(*sources)


def gate_kernel(*refs):
    pass


def gate(array, deps, flops=1):
    hbm = pl.BlockSpec(memory_space=pltpu.HBM)
    return pl.pallas_call(
        gate_kernel,
        in_specs=[hbm] * (1 + len(deps)),
        out_specs=hbm,
        out_shape=jax.ShapeDtypeStruct(array.shape, array.dtype),
        input_output_aliases={0: 0},
        compiler_params=pltpu.CompilerParams(vmem_limit_bytes=VMEM_LIMIT),
        cost_estimate=pl.CostEstimate(flops=flops, transcendentals=0, bytes_accessed=1),
        name="gate",
    )(array, *deps)


def is_odd():
    return lax.axis_index("seq") % 2 == 1


def choose_kernel(odd_ref, even_ref, out):
    @pl.when(is_odd())
    def _():
        out[...] = odd_ref[...]

    @pl.when(jnp.logical_not(is_odd()))
    def _():
        out[...] = even_ref[...]


def merge_kernel(far, got, *refs):
    out = refs[-1]
    out[...] = far[...]

    @pl.when(is_odd())
    def _():
        out[...] = (far[...].astype(F32) + got[...].astype(F32)).astype(BF16)


def join_kernel(dq, own, got, back, *refs):
    out = refs[-1]
    width = dq.shape[1]
    out[:, :width] = dq[...]
    total = own[...] + back[...].astype(F32)

    @pl.when(is_odd())
    def _():
        out[:, width:] = total.astype(BF16)

    @pl.when(jnp.logical_not(is_odd()))
    def _():
        out[:, width:] = (total + got[...].astype(F32)).astype(BF16)


def small(kernel, arrays, deps, width, name, limit=6 * 2**20, cost=1):
    vmem = pl.BlockSpec(memory_space=pltpu.VMEM)
    hbm = pl.BlockSpec(memory_space=pltpu.HBM)
    return pl.pallas_call(
        kernel,
        in_specs=[vmem] * len(arrays) + [hbm] * len(deps),
        out_specs=vmem,
        out_shape=jax.ShapeDtypeStruct((arrays[0].shape[0], width), BF16),
        compiler_params=pltpu.CompilerParams(vmem_limit_bytes=limit),
        cost_estimate=pl.CostEstimate(flops=cost, transcendentals=0, bytes_accessed=1),
        name=name,
    )(*arrays, *deps)


def shifted(array, by):
    peers = lax.axis_size("seq")
    pairs = [(i, i + by) for i in range(peers) if 0 <= i + by < peers]
    return lax.ppermute(array, "seq", pairs)


def swapped(array, bits):
    peers = lax.axis_size("seq")
    return lax.ppermute(array, "seq", [(i, i ^ bits) for i in range(peers)])


def layered(array, moves):
    pairs = [(a * INNER + i, b * INNER + i) for a, b in moves for i in range(INNER)]
    return lax.ppermute(array, "seq", pairs)


def crossed(array, layers, inward):
    pairs = []
    for i in range(layers * INNER):
        half = i // INNER // (layers // 2)
        pairs.append((2 * i + 1 - half, 2 * i + half) if inward else (2 * i + half, 2 * i + 1 - half))
    return lax.ppermute(array, ("seq", "head"), pairs)


def returned(blocks):
    return [blocks[0], swapped(blocks[2], 1), swapped(blocks[1], 2), swapped(blocks[3], 3)]


def ordered(blocks, inner):
    cols = []
    for j in range(INNER):
        pick = blocks[j]
        for i in range(1, INNER):
            pick = jnp.where(inner == i, blocks[j ^ i], pick)
        cols.append(pick)
    return jnp.concatenate(cols, 1)


def project_gathered(grads, weight, layers, tokens, head, inner):
    rows = weight.shape[0]
    groups = [[z * INNER + i for z in range(layers)] for i in range(INNER)]
    every = lax.all_gather(weight, "seq", axis=0, tiled=True, axis_index_groups=groups)
    halves = every.reshape(2, layers // 2 * rows, -1)

    def times(piece):
        return lax.dot_general(
            grads, piece, (((1,), (1,)), ((), ())), preferred_element_type=F32
        )

    send = times(jnp.where(head == 0, halves[1], halves[0])).astype(BF16)
    got = lax.ppermute(send, "head", [(0, 1), (1, 0)])
    keep = times(jnp.where(head == 0, halves[0], halves[1]))
    blocks = returned((keep + got.astype(F32)).astype(BF16).reshape(INNER, tokens, -1))
    blocks = [b.reshape(tokens * (layers // 2), rows) for b in blocks]
    return ordered(blocks, inner).reshape(tokens, -1)


def tied(*arrays):
    return lax.optimization_barrier(arrays)


def shards(
    query, key, value, output, output_gradient, lse, doc_lengths, w_query, key_weight, value_weight
):
    tokens = query.shape[0]
    seq = lax.axis_index("seq")
    head = lax.axis_index("head")
    inner = seq % INNER
    layers = lax.axis_size("seq") // INNER
    line = layers == 4

    rows = w_query.shape[0]
    if line:
        pair, weight = pack((key, value), (w_query, key_weight, value_weight))
    else:
        pair = jnp.concatenate([key, value], 1)
        weight = jnp.concatenate([w_query, key_weight, value_weight], 1)
    pair_width = pair.shape[1]
    far = shifted(pair, 2)
    near = swapped(small(choose_kernel, [far, pair], [], pair.shape[1], "choose"), 1)
    if line:
        up = layered(weight, [(0, 1), (1, 2), (2, 3)])
        down = layered(weight, [(1, 0), (2, 1), (3, 2)])
    first = (seq * tokens).astype(jnp.int32).reshape(1)
    groups = key.shape[1] // HEAD_SIZE
    dq, earlier = [], []
    for g in range(groups):
        dq_part, *parts = attention(
            g, ATTENTION_COST, first, doc_lengths, query, output_gradient, output, lse,
            pair, near, far, earlier,
        )
        dq.append(dq_part)
        earlier += parts
    own_part, near_part, far_part = parts
    dq_y = [swapped(part, 2) for part in dq[:-1]]
    if line:
        down = gate(down, dq_y)
        up_on = layered(up, [(1, 2), (2, 3)])
        down_on = layered(down, [(1, 0), (2, 1)])
    got = swapped(near_part, 1)
    back = shifted(small(merge_kernel, [far_part, got], [], pair.shape[1], "merge"), -2)
    deps = [up, down] if line else []
    width = dq[-1].shape[1] + pair.shape[1]
    joined = small(
        join_kernel, [dq[-1], own_part, got, back], deps, width, "join", VMEM_LIMIT, JOIN_COST
    )
    joined_y = swapped(joined, 2)
    grads = [*dq[:-1], joined, *dq_y, joined_y]
    others = [swapped(g, 1) for g in grads]
    grads = grads + others

    if not line:
        parts = len(grads) // INNER
        four = jnp.concatenate(
            [jnp.concatenate(grads[t * parts : (t + 1) * parts], 1) for t in range(INNER)], 0
        )
        return project_gathered(four, weight, layers, tokens, head, inner)

    early = [o for o, g in zip(others, grads) if g is not joined and g is not joined_y]
    weight = gate(weight, [up_on, down_on, joined_y, *early])
    last = layered(weight, [(0, 3), (3, 0)])
    mate, third = [down, up, down, up], [down_on, down, up, up_on]
    late = [last, down_on, up_on, last]
    send, held = project_send(layers, grads, weight, third)
    got = lax.ppermute(send, "head", [(0, 1), (1, 0)])
    keep, mate_full, mate_low = project_keep(layers, held, weight, mate, third, [send])
    got_mate = crossed(mate_low, layers, True)
    order = (1, 3, 0, 2)
    last_full, *lows = project_last(order, layers, held, late, [got])
    gots = [crossed(low, layers, False) for low in lows]

    def lanes(array, k):
        return array[:, k * rows : (k + 1) * rows].astype(F32)

    sets = [returned([(keep[r] + lanes(got, r)).astype(BF16) for r in range(INNER)])]
    blocks, after = [None] * INNER, sets[0][2:3]
    for k, picks in enumerate((order[:2], order[2:])):
        after = combine(layers, order, picks, last_full, mate_full, got_mate, gots[: k + 1], after)
        for r, block in zip(picks, after):
            blocks[r] = block
    sets.append(returned(blocks))
    tasks = [*((0, r) for r in range(INNER)), (1, 2), (1, 3), (1, 0), (1, 1)]
    blocks = [sets[which][r] for which, r in tasks]
    partly = place(layers, tasks[:-2], blocks[:-2], [], 4 * 10**9)
    return place(layers, tasks[-2:], blocks[-2:], [partly], 1)


def solution(mesh):
    in_specs = (
        P("seq", "head"),
        P("seq", "head"),
        P("seq", "head"),
        P("seq", "head"),
        P("seq", "head"),
        P("head", "seq"),
        P(),
        P("seq", "head"),
        P("seq", "head"),
        P("seq", "head"),
    )
    out_specs = P("seq", "head")
    return jax.shard_map(shards, mesh=mesh, in_specs=in_specs, out_specs=out_specs, check_vma=False)
```
